32 devices in a mesh: vir: 4 (over z), occ: 2 (over x), ka: 4 (over y, core).
Axes of the slice: x: 2, y: 2, z: 4, core: 2. Of those that a mesh axis runs over, the one named last changes fastest.
Arguments:
- ladder_amplitudes: bfloat16 [512, 53248], P('vir', ('occ', 'ka')), may hold values from -6 to 6
- ladder_integrals: bfloat16 [53248, 8192], P(('occ', 'ka'), 'vir'), may hold values from -0.02734375 to 0.02734375
- cycle_amplitudes: bfloat16 [8, 8, 640, 5120], P('occ', 'vir', None, 'ka'), may hold values from -6 to 6
- cycle_integrals: bfloat16 [8, 5120, 8, 640], P('occ', 'ka', 'vir'), may hold values from -0.078125 to 0.078125
Outputs:
- ladder_residual: bfloat16 [512, 8192], P(('occ', 'ka'), 'vir')
- cycle_residual: bfloat16 [8, 8, 640, 8, 640], P('occ', 'vir', 'ka')
The draws below stay inside these ranges and needn't reach their ends.
All inputs are finite; a program needn't handle non-finite values.
Results may differ from the reference program's by a relative error of at most 0.02.
Values may be sent and summed in bfloat16 or wider, within the bound.
No kernel may reach another device: no remote copies, remote signals or barrier semaphores. Data moves between devices by JAX's collectives and lax.ppermute only.
A program may use at most 256 MiB of HBM per device.

```python
import jax
import jax.numpy as jnp
from jax import lax

OP = 512
CD = 53248
AB = 8192
GRP = 640
OVG = 5120
N_KA = 4


def raised(entries, stream_key, source, target, shards_of, factor):
    owner, partner = [(jnp.arange(entries.shape[position]) // (entries.shape[position] // shards_of)).reshape([-1 if axis == position else 1 for axis in range(entries.ndim)]) for position in (source, target)]
    chosen = jax.random.permutation(stream_key, shards_of)[partner]
    strong = (owner == chosen) | (owner == (partner + shards_of // 2) % shards_of)
    return jnp.where(strong, factor * entries, entries)


def levels(rng, extent, shards, low, top_value):
    level = 1.0
    for position, blocks in shards:
        steps = jax.random.uniform(jax.random.fold_in(jax.random.fold_in(rng, 6), position), (blocks,), jnp.float32, low / len(shards), top_value / len(shards))
        level = level * jnp.repeat(jnp.exp(steps), extent[position] // blocks).reshape((-1,) + (1,) * (len(extent) - 1 - position))
    return level


def scatter_about(stream_key, extent, width, reach, shards=(), held_as=jnp.bfloat16):
    loudness = levels(stream_key, extent, shards, -0.22, 0.18) if shards else 1.0
    values = jax.random.normal(stream_key, extent, jnp.float32) * width * loudness
    return jnp.minimum(jnp.maximum(values, -reach), reach).astype(held_as)


def heavy_noise(key, shape, spread, reach, split, heavy, held_as=jnp.bfloat16):
    values = spread * jax.random.normal(key, shape, jnp.float32)
    if split:
        values = values * levels(key, shape, split, -0.22, 0.18)
    return jnp.clip(raised(values, jax.random.fold_in(key, 3), *heavy), -reach, reach).astype(held_as)


def setup_inputs(seed: int = 0) -> dict:
    seeds = jax.random.split(jax.random.key(seed), 5)
    return {
        "ladder_amplitudes": heavy_noise(seeds[0], (OP, CD), 1.0, 6.0, ((0, 4), (1, 8)), (1, 0, 8, 2.0)),
        "ladder_integrals": scatter_about(seeds[1], (CD, AB), CD ** -0.5, 0.02734375, ((0, 8), (1, 4))),
        "cycle_amplitudes": heavy_noise(seeds[2], (8, 8, GRP, OVG), 1.0, 6.0, ((0, 2), (1, 4), (3, 4)), (3, 2, 4, 2.0)),
        "cycle_integrals": scatter_about(seeds[3], (8, OVG, 8, GRP), OVG ** -0.5, 0.078125, ((0, 2), (1, 4), (2, 4))),
    }


def cycle_one_irrep(operands):
    amplitudes, integrals = operands
    quarter = (8 * GRP) // N_KA
    total = jnp.zeros((8, GRP, 8, GRP), jnp.float32)
    for quarter_index in range(N_KA):
        left = amplitudes[:, :, quarter_index * quarter:(quarter_index + 1) * quarter].astype(jnp.float32)
        right = integrals[quarter_index * quarter:(quarter_index + 1) * quarter].astype(jnp.float32)
        term = jnp.einsum("axk,kny->axny", left, right)
        rounded = lax.optimization_barrier(term.astype(jnp.bfloat16))
        total = total + rounded.astype(jnp.float32)
    return total.astype(jnp.bfloat16)


def reference(ladder_amplitudes, ladder_integrals, cycle_amplitudes, cycle_integrals):
    ladder_residual = jnp.dot(ladder_amplitudes, ladder_integrals, preferred_element_type=jnp.float32).astype(jnp.bfloat16)
    blocks = lax.map(cycle_one_irrep, (cycle_amplitudes, cycle_integrals))
    irreps = jnp.arange(8, dtype=jnp.int32)
    partner = jnp.bitwise_xor(irreps[:, None], irreps[None, :])
    row_irrep = jnp.broadcast_to(irreps[None, :], (8, 8))
    picked = blocks[:, row_irrep, :, partner, :]
    cycle_residual = jnp.transpose(picked, (0, 1, 3, 2, 4))
    return ladder_residual, cycle_residual
```

```python
import jax
import jax.numpy as jnp
from jax import lax
from jax.experimental import pallas as pl
from jax.experimental.pallas import tpu as pltpu
from jax.sharding import PartitionSpec as P

F32, BF16 = jnp.float32, jnp.bfloat16

END_TO_MID = [(0, 1), (3, 2)]
MID_TO_MID = [(1, 2), (2, 1)]
MID_TO_END = [(1, 0), (2, 3)]
RELATIVE = (0, 2, 1, 3)
OTHER_CORE = [(0, 1), (1, 0), (2, 3), (3, 2)]
OTHER_Y = [(0, 2), (2, 0), (1, 3), (3, 1)]
OTHER_OCC = [(0, 1), (1, 0)]
ROOM = 60 << 20
CHEAP = pl.CostEstimate(flops=1 << 20, bytes_accessed=1 << 16, transcendentals=0)


def after(value, *earlier):
    return lax.optimization_barrier((value, *earlier))[0]


def dot_rows(lhs, rhs):
    return jnp.dot(lhs.reshape(-1, lhs.shape[-1]), rhs, preferred_element_type=F32)


def lhs_specs(irrep, sources, rows, depth, first):
    specs = []
    for place in range(sources):
        def quarter(s, r, where, place=place):
            moment = r if sources == 1 else jnp.where(s == place, r, 1 if place == 0 else 0)
            return where[first + moment]
        if place == 0:
            specs.append(pl.BlockSpec((1, 2, rows, depth), lambda s, r, where, q=quarter: (irrep, 0, q(s, r, where), 0)))
        else:
            specs.append(pl.BlockSpec((2, rows, depth), lambda s, r, where, q=quarter: (0, q(s, r, where), 0)))
    return specs


def product(lhs_refs, rhs_ref, use):
    source = pl.program_id(0)
    for place, lhs in enumerate(lhs_refs):
        @pl.when(source == place)
        def _():
            use(dot_rows(lhs[...], rhs_ref[...]))


def send_product(where, irrep, lhs, rhs):
    sources, depth, columns = len(lhs), rhs.shape[0], rhs.shape[1]
    rows = lhs[0].shape[2] // 4

    def kernel(where_ref, *refs):
        out = refs[-1]

        def use(value):
            out[0, 0] = value.astype(BF16)
        product(refs[:sources], refs[sources], use)

    return pl.pallas_call(
        kernel,
        out_shape=jax.ShapeDtypeStruct((sources, 2, 2 * rows, columns), BF16),
        grid_spec=pltpu.PrefetchScalarGridSpec(
            num_scalar_prefetch=1,
            grid=(sources, 2),
            in_specs=lhs_specs(irrep, sources, rows, depth, 2)
            + [pl.BlockSpec((depth, columns), lambda s, r, where: (0, 0))],
            out_specs=pl.BlockSpec((1, 1, 2 * rows, columns), lambda s, r, where: (s, r, 0, 0)),
        ),
        compiler_params=pltpu.CompilerParams(vmem_limit_bytes=ROOM),
        cost_estimate=CHEAP,
        name="send_product",
    )(where, *lhs, rhs)


def keep_product(where, irrep, lhs, rhs, arrived):
    sources, depth, columns = len(lhs), rhs.shape[0], rhs.shape[1]
    rows = lhs[0].shape[2] // 4

    def kernel(where_ref, *refs):
        arrived_ref, away, own = refs[sources + 1:]
        quarter = pl.program_id(1)

        def use(value):
            total = value + arrived_ref[0, 0].astype(F32)

            @pl.when(quarter == 0)
            def _():
                own[0] = total.astype(BF16)

            @pl.when(quarter == 1)
            def _():
                away[0] = total.astype(BF16)
        product(refs[:sources], refs[sources], use)

    return pl.pallas_call(
        kernel,
        out_shape=(
            jax.ShapeDtypeStruct((sources, 2 * rows, columns), BF16),
            jax.ShapeDtypeStruct((sources, 2 * rows, columns), BF16),
        ),
        grid_spec=pltpu.PrefetchScalarGridSpec(
            num_scalar_prefetch=1,
            grid=(sources, 2),
            in_specs=lhs_specs(irrep, sources, rows, depth, 0)
            + [pl.BlockSpec((depth, columns), lambda s, r, where: (0, 0)),
               pl.BlockSpec((1, 1, 2 * rows, columns), lambda s, r, where: (s, r, 0, 0))],
            out_specs=(pl.BlockSpec((1, 2 * rows, columns), lambda s, r, where: (s, 0, 0)),) * 2,
        ),
        compiler_params=pltpu.CompilerParams(vmem_limit_bytes=ROOM),
        cost_estimate=CHEAP,
        name="keep_product",
    )(where, *lhs, rhs, arrived)


def whole_product(irrep, products):
    count = len(products)
    lhs, rhs = zip(*products)
    depth, columns = lhs[0].shape[-1], rhs[0][0].shape[-1]
    rows = lhs[0].shape[-2] // 4

    def kernel(*refs):
        out = refs[-1]
        for index in range(count):
            @pl.when(pl.program_id(0) == index)
            def _():
                out[0, 0] = dot_rows(refs[index][...], refs[count + index][...]).astype(BF16)

    specs = []
    for index, array in enumerate(lhs):
        def quarter(p, r, index=index):
            return jnp.where(p == index, r, jnp.where(p < index, 0, 3))
        if array.ndim == 4:
            specs.append(pl.BlockSpec((1, 2, rows, depth), lambda p, r, q=quarter: (irrep, 0, q(p, r), 0)))
        else:
            specs.append(pl.BlockSpec((2, rows, depth), lambda p, r, q=quarter: (0, q(p, r), 0)))
    for array, index in rhs:
        specs.append(pl.BlockSpec((depth, columns), lambda p, r, index=index: (index, 0)))
    return pl.pallas_call(
        kernel,
        out_shape=jax.ShapeDtypeStruct((4, count, 2 * rows, columns), BF16),
        grid=(count, 4),
        in_specs=specs,
        out_specs=pl.BlockSpec((1, 1, 2 * rows, columns), lambda p, r: (r, p, 0, 0)),
        compiler_params=pltpu.CompilerParams(vmem_limit_bytes=ROOM),
        cost_estimate=CHEAP,
        name="whole_product",
    )(*lhs, *[array for array, _ in rhs])


def place(base, parity, kept, arrived, out, shape):
    count = len(kept)
    rows, columns = shape[2], shape[4]
    block = rows // 2

    def kernel(base_ref, *refs):
        out_ref, wide = refs[-2:]
        first = base_ref[1] == 0
        for index in range(count):
            mine, theirs = refs[index][0].astype(F32), refs[count + index][0].astype(F32)
            wide[:, index, :] = jnp.where(first, mine, theirs)
            wide[:, count + index, :] = jnp.where(first, theirs, mine)
        out_ref[0, 0] = wide[...].astype(BF16)

    pieces = kept + arrived
    specs = [
        pl.BlockSpec((1, block, columns), lambda a, i, base, j=j, step=array.shape[0] - 2: (
            a + step * (1 - base[1]), i, j))
        for array, j in pieces]
    extra = [] if out is None else [out]
    return pl.pallas_call(
        kernel,
        out_shape=jax.ShapeDtypeStruct(shape, BF16),
        grid_spec=pltpu.PrefetchScalarGridSpec(
            num_scalar_prefetch=1,
            grid=(2, rows // block),
            in_specs=specs + [pl.BlockSpec(memory_space=pl.ANY)] * len(extra),
            out_specs=pl.BlockSpec(
                (1, 1, block, 2 * count, columns),
                lambda a, i, base: (base[0] + (a + parity) % 2, a, i, 0, 0)),
            scratch_shapes=[pltpu.VMEM((block, 2 * count, columns), F32)],
        ),
        input_output_aliases={1 + 2 * count: 0} if extra else {},
        compiler_params=pltpu.CompilerParams(vmem_limit_bytes=ROOM),
        cost_estimate=CHEAP,
        name="place",
    )(base, *[array for array, _ in pieces], *extra)


class Order:
    def __init__(self):
        self.before, self.edge = [], []

    def follow(self, value):
        return after(value, *self.before) if self.before else value

    def step(self, value):
        self.before = [value]
        return value

    def phase(self, *values):
        self.before = self.before + list(values)
        self.edge = self.before

    def open(self, value):
        return after(value, *self.edge) if self.edge else value


class Task:
    def __init__(self, order, where, irrep, lhs, rhs):
        self.order, self.where, self.irrep, self.lhs, self.rhs = order, where, irrep, lhs, rhs

    def send(self):
        self.rhs = self.order.follow(self.rhs)
        part = self.order.step(send_product(self.where, self.irrep, self.lhs, self.rhs))
        self.arrived = lax.ppermute(part, "ka", OTHER_CORE)

    def keep(self):
        arrived = self.order.follow(self.arrived)
        away, self.own = keep_product(self.where, self.irrep, self.lhs, self.rhs, arrived)
        self.order.step(away)
        self.other = lax.ppermute(away, "ka", OTHER_Y)

    def finish(self):
        other = self.order.follow(self.other)
        total = (self.own.astype(F32) + other.astype(F32)).astype(BF16)
        self.order.step(total)
        sources, rows, columns = total.shape
        self.parts = [total[s].reshape(2, rows // 2, columns) for s in range(sources)]


def line_local(ladder_amplitudes, ladder_integrals, cycle_amplitudes, cycle_integrals):
    vir, occ, ka = (lax.axis_index(name) for name in ("vir", "occ", "ka"))
    irreps, rows_here, group, depth = cycle_amplitudes.shape
    quarter = group // 4
    columns = cycle_integrals.shape[3]
    at_end = (vir == 0) | (vir == 3)
    where = jnp.bitwise_xor(ka, jnp.array(RELATIVE, jnp.int32))
    order = Order()

    def columns_of(g):
        return order.open(cycle_integrals[g]).reshape(depth, 2 * columns)

    def task(g, rhs, foreign=None):
        lhs = (cycle_amplitudes,) if foreign is None else (cycle_amplitudes, foreign)
        return Task(order, where, g, lhs, rhs)

    def move(value, route):
        return lax.ppermute(order.open(value), "vir", route)

    def scatter(products, g):
        part = order.step(whole_product(g, [(lhs, (order.follow(rhs), index)) for lhs, (rhs, index) in products]))
        total = lax.psum_scatter(part, "ka", scatter_dimension=0, tiled=True)
        return total.reshape(len(products), 2, quarter, 2 * columns)

    def cross(near, far, by_gather=False):
        away = order.open(jnp.where(occ == 0, far, near))
        if by_gather:
            arrived = lax.all_gather(away, "occ", axis=0, tiled=True)
        else:
            arrived = lax.ppermute(away, "occ", OTHER_OCC)
        return jnp.where(occ == 0, near, far), arrived

    def home(mine, back):
        return jnp.where(at_end, back, mine)

    low = jnp.where((occ == 0) | at_end, 0, 2).astype(jnp.int32)
    shape = (8 // 2, rows_here, quarter, 2 * irreps, columns)

    def put(half, j, crossed, out):
        base = jnp.stack([low if half == 0 else 2 - low, occ.astype(jnp.int32)])
        kept = [(pair[0], jj) for pair, jj in crossed]
        arrived = [(pair[1], jj) for pair, jj in crossed]
        return order.step(place(base, j, kept, arrived, out, shape))

    ca = cycle_amplitudes
    b0 = columns_of(0)
    own0 = move(b0, MID_TO_MID)
    a0 = move(ca[0], END_TO_MID)
    b3 = columns_of(3)
    all3 = lax.all_gather(b3, "vir", axis=0, tiled=True)
    b0_in = move(b0, END_TO_MID)
    b1, b2 = columns_of(1), columns_of(2)

    order.phase(own0, a0, b0_in, b1, b2)
    own1 = move(b1, MID_TO_MID)
    a1 = move(ca[1], END_TO_MID)
    f0 = task(0, own0, a0)
    f0.send()
    s0 = scatter([(ca, (b0, 0)), (a0, (b0, 0))], 0)
    f0.keep()
    n0 = scatter([(ca, (b0_in, 0))], 0)
    f0.finish()

    order.phase(own1, a1, all3)
    relay0 = move(b0_in, MID_TO_MID)
    b1_in = move(b1, END_TO_MID)
    f0_back = move(f0.parts[1], MID_TO_END)
    gathered = lax.all_gather(order.open(ladder_amplitudes), "vir", axis=0, tiled=True)
    f1 = task(1, own1, a1)
    f1.send()
    s1 = scatter([(ca, (b1, 0)), (a1, (b1, 0))], 1)
    f1.keep()
    t3 = scatter([(ca, (all3, w)) for w in range(4)], 3)
    f1.finish()

    order.phase(relay0, b1_in, f0_back, s0, n0)
    own2 = move(b2, MID_TO_MID)
    a2 = move(ca[2], END_TO_MID)
    f1_back = move(f1.parts[1], MID_TO_END)
    s0_back = move(s0[1], MID_TO_END)
    g0 = task(0, relay0, a0)
    g0.send()
    n1 = scatter([(ca, (b1_in, 0))], 1)
    g0.keep()
    g0.finish()

    order.phase(own2, a2, f1_back, s0_back, s1, gathered)
    relay1 = move(b1_in, MID_TO_MID)
    b2_in = move(b2, END_TO_MID)
    g0_back = move(g0.parts[1], MID_TO_END)
    s1_back = move(s1[1], MID_TO_END)
    x0a = cross(s0[0], home(f0.parts[0], f0_back), True)
    x1a = cross(s1[0], home(f1.parts[0], f1_back), True)
    f2 = task(2, own2, a2)
    f2.send()
    s2 = scatter([(ca, (b2, 0)), (a2, (b2, 0))], 2)
    f2.keep()
    partial_ladder = order.step(jnp.dot(
        order.follow(gathered), ladder_integrals, preferred_element_type=F32,
    ).astype(BF16))
    ladder_residual = lax.psum_scatter(partial_ladder, ("occ", "ka"), scatter_dimension=0, tiled=True)
    f2.finish()

    order.phase(relay1, b2_in, g0_back, s1_back, n1, t3, x0a[1], x1a[1])
    relay2 = [move(b2_in[:, j * columns:(j + 1) * columns], MID_TO_MID) for j in range(2)]
    f2_back = move(f2.parts[1], MID_TO_END)
    middle = vir // 2
    near3, next3, far3, last3 = (
        lax.dynamic_index_in_dim(t3, w, 0, keepdims=False)
        for w in (vir, vir + 1 - 2 * (vir % 2), 2 - middle, 3 - 3 * middle))
    x3a = cross(near3, far3, True)
    x0b = cross(home(n0[0], s0_back), home(g0.parts[0], g0_back), True)
    g1 = task(1, relay1, a1)
    g1.send()
    n2 = scatter([(ca, (b2_in, 0))], 2)
    g1.keep()
    x3b = cross(next3, last3)
    g1.finish()

    order.phase(relay2[0], f2_back, x3a[1], x0b[1], x3b[1], s2)
    g1_back = move(g1.parts[1], MID_TO_END)
    s2_back = move(s2[1], MID_TO_END)
    x2a = cross(s2[0], home(f2.parts[0], f2_back))
    g2 = [task(2, value, a2) for value in relay2]
    g2[0].send()
    g2[0].keep()
    g2[1].send()
    g2[1].keep()
    order.phase(g1_back, s2_back, x2a[1], n2, ladder_residual)
    x1b = cross(home(n1[0], s1_back), home(g1.parts[0], g1_back))
    out = put(0, 0, [(x0a, 0), (x1a, 0), (x2a, 0), (x3a, 0)], None)
    g2[0].finish()
    back = [move(g2[0].parts[1], MID_TO_END)]
    out = put(0, 1, [(x0a, 1), (x1a, 1), (x2a, 1), (x3a, 1)], out)
    g2[1].finish()
    back.append(move(g2[1].parts[1], MID_TO_END))
    near = home(n2[0], s2_back)
    x2b = [
        cross(near[..., j * columns:(j + 1) * columns], home(g2[j].parts[0], back[j])) for j in range(2)]
    for j in range(2):
        out = put(1, j, [(x0b, j), (x1b, j), (x2b[j], 0), (x3b, j)], out)
    return ladder_residual, out


def regroup(blocks):
    local_rows = blocks.shape[1]
    first_irrep = lax.axis_index("vir") * local_rows
    pieces = []
    for local_index in range(local_rows):
        permuted = jnp.bitwise_xor(first_irrep + local_index, jnp.arange(8, dtype=jnp.int32))
        pieces.append(jnp.take(blocks[:, local_index], permuted, axis=2))
    stacked = jnp.stack(pieces, axis=1)
    return jnp.transpose(stacked, (3, 1, 2, 0, 4))


def any_local(ladder_amplitudes, ladder_integrals, cycle_amplitudes, cycle_integrals):
    partial_ladder = jnp.dot(
        lax.all_gather(ladder_amplitudes, "vir", axis=0, tiled=True),
        ladder_integrals,
        preferred_element_type=F32,
    )
    summed_ladder = lax.psum_scatter(
        partial_ladder.astype(BF16), ("occ", "ka"), scatter_dimension=0, tiled=True
    )
    partial_cycle = jnp.einsum(
        "gaxk,gkny->gaxny",
        cycle_amplitudes,
        lax.all_gather(cycle_integrals, "vir", axis=2, tiled=True),
        preferred_element_type=F32,
    )
    summed_cycle = lax.psum_scatter(
        partial_cycle.astype(BF16), "ka", scatter_dimension=2, tiled=True
    )
    arranged = regroup(summed_cycle)
    cycle_residual = lax.all_to_all(arranged, "occ", split_axis=0, concat_axis=3, tiled=True)
    return (summed_ladder, cycle_residual)


def solution(mesh):
    line = (mesh.shape["vir"], mesh.shape["occ"], mesh.shape["ka"]) == (4, 2, 4)
    placed = (
        P("vir", ("occ", "ka")),
        P(("occ", "ka"), "vir"),
        P("occ", "vir", None, "ka"),
        P("occ", "ka", "vir", None),
    )
    return jax.shard_map(
        line_local if line else any_local,
        mesh=mesh,
        in_specs=placed,
        out_specs=(P(("occ", "ka"), "vir"), P("occ", "vir", "ka", None, None)),
        check_vma=False,
    )
```

```python
import jax
import jax.numpy as jnp
from jax import lax
from jax.experimental import pallas as pl
from jax.experimental.pallas import tpu as pltpu
from jax.sharding import PartitionSpec as P

F32, BF16 = jnp.float32, jnp.bfloat16

END_TO_MID = [(0, 1), (3, 2)]
MID_TO_MID = [(1, 2), (2, 1)]
MID_TO_END = [(1, 0), (2, 3)]
RELATIVE = (0, 2, 1, 3)
OTHER_CORE = [(0, 1), (1, 0), (2, 3), (3, 2)]
OTHER_Y = [(0, 2), (2, 0), (1, 3), (3, 1)]
OTHER_OCC = [(0, 1), (1, 0)]
NEIGHBOUR = [(0, 1), (1, 0), (2, 3), (3, 2)]
ROOM = 60 << 20
CHEAP = pl.CostEstimate(flops=1 << 20, bytes_accessed=1 << 16, transcendentals=0)


def after(value, *earlier):
    return lax.optimization_barrier((value, *earlier))[0]


def dot_rows(lhs, rhs):
    return jnp.dot(lhs.reshape(-1, lhs.shape[-1]), rhs, preferred_element_type=F32)


def lhs_specs(irrep, sources, rows, depth, first):
    specs = []
    for place in range(sources):
        def quarter(s, r, where, place=place):
            moment = r if sources == 1 else jnp.where(s == place, r, 1 if place == 0 else 0)
            return where[first + moment]
        if place == 0:
            specs.append(pl.BlockSpec((1, 2, rows, depth), lambda s, r, where, q=quarter: (irrep, 0, q(s, r, where), 0)))
        else:
            specs.append(pl.BlockSpec((2, rows, depth), lambda s, r, where, q=quarter: (0, q(s, r, where), 0)))
    return specs


def product(lhs_refs, rhs_ref, use):
    source = pl.program_id(0)
    for place, lhs in enumerate(lhs_refs):
        @pl.when(source == place)
        def _():
            use(place, dot_rows(lhs[...], rhs_ref[...]))


def quarter_specs(sources, rows, columns):
    def at(place):
        return lambda s, r, where: (r if sources == 1 else jnp.where(s == place, r, 1 - place), 0, 0)
    return [pl.BlockSpec((1, rows, columns), at(place)) for place in range(sources)]


def send_product(where, irrep, lhs, rhs):
    sources, depth, columns = len(lhs), rhs.shape[0], rhs.shape[1]
    rows = lhs[0].shape[2] // 4

    def kernel(where_ref, *refs):
        outs = refs[sources + 1:]

        def use(place, value):
            outs[place][0] = value.astype(BF16)
        product(refs[:sources], refs[sources], use)

    return pl.pallas_call(
        kernel,
        out_shape=[jax.ShapeDtypeStruct((2, 2 * rows, columns), BF16)] * sources,
        grid_spec=pltpu.PrefetchScalarGridSpec(
            num_scalar_prefetch=1,
            grid=(sources, 2),
            in_specs=lhs_specs(irrep, sources, rows, depth, 2)
            + [pl.BlockSpec((depth, columns), lambda s, r, where: (0, 0))],
            out_specs=quarter_specs(sources, 2 * rows, columns),
        ),
        compiler_params=pltpu.CompilerParams(vmem_limit_bytes=ROOM),
        cost_estimate=CHEAP,
        name="send_product",
    )(where, *lhs, rhs)


def keep_product(where, irrep, lhs, rhs, arrived):
    sources, depth, columns = len(lhs), rhs.shape[0], rhs.shape[1]
    rows = lhs[0].shape[2] // 4

    def kernel(where_ref, *refs):
        arrived_refs, (away, own) = refs[sources + 1:-2], refs[-2:]
        quarter = pl.program_id(1)

        def use(place, value):
            total = (value + arrived_refs[place][0].astype(F32)).astype(BF16)

            @pl.when(quarter == 0)
            def _():
                own[0] = total

            @pl.when(quarter == 1)
            def _():
                away[0] = total
        product(refs[:sources], refs[sources], use)

    return pl.pallas_call(
        kernel,
        out_shape=(jax.ShapeDtypeStruct((sources, 2 * rows, columns), BF16),) * 2,
        grid_spec=pltpu.PrefetchScalarGridSpec(
            num_scalar_prefetch=1,
            grid=(sources, 2),
            in_specs=lhs_specs(irrep, sources, rows, depth, 0)
            + [pl.BlockSpec((depth, columns), lambda s, r, where: (0, 0))]
            + quarter_specs(sources, 2 * rows, columns),
            out_specs=(pl.BlockSpec((1, 2 * rows, columns), lambda s, r, where: (s, 0, 0)),) * 2,
        ),
        compiler_params=pltpu.CompilerParams(vmem_limit_bytes=ROOM),
        cost_estimate=CHEAP,
        name="keep_product",
    )(where, *lhs, rhs, *arrived)


def place(base, parity, kept, arrived, out, shape):
    count = len(kept)
    rows, columns = shape[2], shape[4]
    block = rows // 2

    def kernel(base_ref, *refs):
        out_ref, wide = refs[-2:]
        first = base_ref[1] == 0
        for index in range(count):
            mine, theirs = refs[index][0].astype(F32), refs[count + index][0].astype(F32)
            wide[:, index, :] = jnp.where(first, mine, theirs)
            wide[:, count + index, :] = jnp.where(first, theirs, mine)
        out_ref[0, 0] = wide[...].astype(BF16)

    pieces = kept + arrived
    specs = [
        pl.BlockSpec((1, block, columns), lambda a, i, base, j=j, step=array.shape[0] - 2: (
            a + step * (1 - base[1]), i, j))
        for array, j in pieces]
    extra = [] if out is None else [out]
    return pl.pallas_call(
        kernel,
        out_shape=jax.ShapeDtypeStruct(shape, BF16),
        grid_spec=pltpu.PrefetchScalarGridSpec(
            num_scalar_prefetch=1,
            grid=(2, rows // block),
            in_specs=specs + [pl.BlockSpec(memory_space=pl.ANY)] * len(extra),
            out_specs=pl.BlockSpec(
                (1, 1, block, 2 * count, columns),
                lambda a, i, base: (base[0] + (a + parity) % 2, a, i, 0, 0)),
            scratch_shapes=[pltpu.VMEM((block, 2 * count, columns), F32)],
        ),
        input_output_aliases={1 + 2 * count: 0} if extra else {},
        compiler_params=pltpu.CompilerParams(vmem_limit_bytes=ROOM),
        cost_estimate=CHEAP,
        name="place",
    )(base, *[array for array, _ in pieces], *extra)


class Order:
    def __init__(self):
        self.before, self.edge = [], []

    def follow(self, value):
        return after(value, *self.before) if self.before else value

    def step(self, value):
        self.before = [value]
        return value

    def phase(self, *values):
        self.before = self.before + list(values)
        self.edge = self.before

    def open(self, value):
        return after(value, *self.edge) if self.edge else value


class Task:
    def __init__(self, order, where, irrep, lhs, rhs):
        self.order, self.where, self.irrep, self.lhs, self.rhs = order, where, irrep, lhs, rhs

    def send(self):
        self.rhs = self.order.follow(self.rhs)
        parts = send_product(self.where, self.irrep, self.lhs, self.rhs)
        self.order.step(parts[-1])
        self.arrived = [lax.ppermute(part, "ka", OTHER_CORE) for part in parts]

    def keep(self):
        arrived = [self.order.follow(part) for part in self.arrived]
        self.away, self.own = keep_product(self.where, self.irrep, self.lhs, self.rhs, arrived)
        self.order.step(self.away)

    def swap(self):
        self.other = lax.ppermute(self.order.open(self.away), "ka", OTHER_Y)

    def finish(self):
        other = self.order.follow(self.other)
        total = (self.own.astype(F32) + other.astype(F32)).astype(BF16)
        self.order.step(total)
        sources, rows, columns = total.shape
        self.parts = [total[s].reshape(2, rows // 2, columns) for s in range(sources)]


def line_local(ladder_amplitudes, ladder_integrals, cycle_amplitudes, cycle_integrals):
    vir, occ, ka = (lax.axis_index(name) for name in ("vir", "occ", "ka"))
    irreps, rows_here, group, depth = cycle_amplitudes.shape
    quarter = group // 4
    columns = cycle_integrals.shape[3]
    at_end = (vir == 0) | (vir == 3)
    where = jnp.bitwise_xor(ka, jnp.array(RELATIVE, jnp.int32))
    order = Order()

    def columns_of(g):
        return order.open(cycle_integrals)[g].reshape(depth, 2 * columns)

    def task(g, rhs, foreign=None):
        lhs = (cycle_amplitudes,) if foreign is None else (cycle_amplitudes, foreign)
        return Task(order, where, g, lhs, rhs)

    def move(value, route):
        return lax.ppermute(order.open(value), "vir", route)

    def cross(near, far):
        away = order.open(jnp.where(occ == 0, far, near))
        return jnp.where(occ == 0, near, far), lax.ppermute(away, "occ", OTHER_OCC)

    def home(mine, back):
        return jnp.where(at_end, back, mine)

    low = jnp.where((occ == 0) | at_end, 0, 2).astype(jnp.int32)
    shape = (8 // 2, rows_here, quarter, 2 * irreps, columns)

    def put(half, j, crossed, out):
        base = jnp.stack([low if half == 0 else 2 - low, occ.astype(jnp.int32)])
        kept = [(pair[0], jj) for pair, jj in crossed]
        arrived = [(pair[1], jj) for pair, jj in crossed]
        return order.step(place(base, j, kept, arrived, out, shape))

    def rows_of(g):
        return order.open(cycle_amplitudes)[g]

    def each(tasks, step):
        for one in tasks:
            getattr(one, step)()

    def straight(near, near_in, done, one=slice(None)):
        own_rows, foreign = (order.open(value) for value in done.parts)
        first = lax.ppermute(jnp.where(occ == 0, own_rows, foreign), ("vir", "occ"), [(2, 3), (4, 5), (3, 1), (5, 7)])
        second = lax.ppermute(foreign, ("vir", "occ"), [(2, 1), (4, 7)])
        kept = jnp.where(occ == 0, near[..., one], jnp.where(at_end, first, own_rows))
        arrived = jnp.where(occ == 0, near_in[..., one], jnp.where(at_end, second, first))
        return kept, arrived

    def over(near):
        return lax.ppermute(order.open(near), "occ", [(1, 0)])

    gathered = lax.all_gather(ladder_amplitudes, "vir", axis=0, tiled=True)
    b0 = columns_of(0)
    order.phase(b0)
    own0 = move(b0, MID_TO_MID)
    a0 = move(rows_of(0), END_TO_MID)
    b3 = columns_of(3)
    s0, s3 = task(0, b0), task(3, b3)
    s0.send()
    s0.keep()
    s3.send()
    s3.keep()

    order.phase(own0, a0)
    own3 = move(b3, MID_TO_MID)
    swap3 = move(b3, NEIGHBOUR)
    each((s0, s3), "swap")
    b1 = columns_of(1)
    f0, s1 = task(0, own0, a0), task(1, b1)
    each((f0, s1), "send")
    each((f0, s1), "keep")
    each((s0, s3), "finish")

    order.phase(own3, swap3, gathered)
    relay3 = move(swap3, MID_TO_MID)
    swap0 = move(b0, NEIGHBOUR)
    each((f0, s1), "swap")
    b2 = columns_of(2)
    n3, s2 = task(3, swap3), task(2, b2)
    each((n3, s2), "send")
    each((n3, s2), "keep")
    each((f0, s1), "finish")

    order.phase(relay3, swap0)
    relay0 = move(swap0, MID_TO_MID)
    a1 = move(rows_of(1), END_TO_MID)
    on3 = move(own3, MID_TO_END)
    f0_back = move(f0.parts[1], MID_TO_END)
    each((n3, s2), "swap")
    n0 = task(0, swap0)
    n0.send()
    n0.keep()
    partial_ladder = order.step(jnp.dot(
        order.follow(gathered), ladder_integrals, preferred_element_type=F32,
    ).astype(BF16))
    ladder_residual = lax.psum_scatter(partial_ladder, ("occ", "ka"), scatter_dimension=0, tiled=True)
    each((n3, s2), "finish")

    order.phase(relay0, a1, on3, f0_back)
    own1 = move(b1, MID_TO_MID)
    a2 = move(rows_of(2), END_TO_MID)
    on_relay3 = move(relay3, MID_TO_END)
    n0.swap()
    x0a = cross(s0.parts[0], home(f0.parts[0], f0_back))
    g0, f3 = task(0, relay0, a0), task(3, jnp.where(at_end, on3, own3))
    each((g0, f3), "send")
    each((g0, f3), "keep")
    n0.finish()

    order.phase(own1, a2, on_relay3, x0a[1])
    own2 = move(b2, MID_TO_MID)
    swap1 = move(b1, NEIGHBOUR)
    each((g0, f3), "swap")
    f1, g3 = task(1, own1, a1), task(3, jnp.where(at_end, on_relay3, relay3))
    each((f1, g3), "send")
    each((f1, g3), "keep")
    each((g0, f3), "finish")

    order.phase(own2, swap1)
    relay1 = move(swap1, MID_TO_MID)
    swap2 = move(b2, NEIGHBOUR)
    g0_back = move(g0.parts[1], MID_TO_END)
    x3a = cross(s3.parts[0], f3.parts[0])
    each((f1, g3), "swap")
    f2, n1 = task(2, own2, a2), task(1, swap1)
    each((f2, n1), "send")
    each((f2, n1), "keep")
    each((f1, g3), "finish")

    order.phase(relay1, swap2, g0_back, x3a[1], ladder_residual)
    relay2 = [move(swap2[:, :columns], MID_TO_MID)]
    f1_back = move(f1.parts[1], MID_TO_END)
    x0b = cross(n0.parts[0], home(g0.parts[0], g0_back))
    each((f2, n1), "swap")
    g1, n2 = task(1, relay1, a1), task(2, swap2)
    each((g1, n2), "send")
    each((g1, n2), "keep")
    each((f2, n1), "finish")

    order.phase(relay2[0], f1_back, x0b[1])
    relay2.append(move(swap2[:, columns:], MID_TO_MID))
    f2_back = move(f2.parts[1], MID_TO_END)
    x1a = cross(s1.parts[0], home(f1.parts[0], f1_back))
    x3b = cross(n3.parts[0], g3.parts[0])
    each((g1, n2), "swap")
    g2 = [task(2, relay2[0], a2)]
    g2[0].send()
    g2[0].keep()
    each((g1, n2), "finish")

    order.phase(relay2[1], f2_back, x1a[1], x3b[1])
    near1_in, near2_in = over(n1.parts[0]), over(n2.parts[0])
    x2a = cross(s2.parts[0], home(f2.parts[0], f2_back))
    g2[0].swap()
    g2.append(task(2, relay2[1], a2))
    g2[1].send()
    g2[1].keep()
    x1b = straight(n1.parts[0], near1_in, g1)
    g2[0].finish()

    order.phase(x2a[1], near2_in, *x1b)
    g2[1].swap()
    out = None
    for j in range(2):
        out = put(0, j, [(x0a, j), (x1a, j), (x2a, j), (x3a, j)], out)
    x2b = [straight(n2.parts[0], near2_in, g2[0], slice(0, columns))]
    g2[1].finish()

    order.phase(*x2b[0])
    x2b.append(straight(n2.parts[0], near2_in, g2[1], slice(columns, 2 * columns)))
    for j in range(2):
        out = put(1, j, [(x0b, j), (x1b, j), (x2b[j], 0), (x3b, j)], out)
    return ladder_residual, out


def regroup(blocks):
    local_rows = blocks.shape[1]
    first_irrep = lax.axis_index("vir") * local_rows
    pieces = []
    for local_index in range(local_rows):
        permuted = jnp.bitwise_xor(first_irrep + local_index, jnp.arange(8, dtype=jnp.int32))
        pieces.append(jnp.take(blocks[:, local_index], permuted, axis=2))
    stacked = jnp.stack(pieces, axis=1)
    return jnp.transpose(stacked, (3, 1, 2, 0, 4))


def any_local(ladder_amplitudes, ladder_integrals, cycle_amplitudes, cycle_integrals):
    partial_ladder = jnp.dot(
        lax.all_gather(ladder_amplitudes, "vir", axis=0, tiled=True),
        ladder_integrals,
        preferred_element_type=F32,
    )
    summed_ladder = lax.psum_scatter(
        partial_ladder.astype(BF16), ("occ", "ka"), scatter_dimension=0, tiled=True
    )
    partial_cycle = jnp.einsum(
        "gaxk,gkny->gaxny",
        cycle_amplitudes,
        lax.all_gather(cycle_integrals, "vir", axis=2, tiled=True),
        preferred_element_type=F32,
    )
    summed_cycle = lax.psum_scatter(
        partial_cycle.astype(BF16), "ka", scatter_dimension=2, tiled=True
    )
    arranged = regroup(summed_cycle)
    cycle_residual = lax.all_to_all(arranged, "occ", split_axis=0, concat_axis=3, tiled=True)
    return (summed_ladder, cycle_residual)


def solution(mesh):
    line = (mesh.shape["vir"], mesh.shape["occ"], mesh.shape["ka"]) == (4, 2, 4)
    placed = (
        P("vir", ("occ", "ka")),
        P(("occ", "ka"), "vir"),
        P("occ", "vir", None, "ka"),
        P("occ", "ka", "vir", None),
    )
    return jax.shard_map(
        line_local if line else any_local,
        mesh=mesh,
        in_specs=placed,
        out_specs=(P(("occ", "ka"), "vir"), P("occ", "vir", "ka", None, None)),
        check_vma=False,
    )
```

```python
import jax
import jax.numpy as jnp
from jax import lax
from jax.experimental import pallas as pl
from jax.experimental.pallas import tpu as pltpu
from jax.sharding import PartitionSpec as P

F32, BF16 = jnp.float32, jnp.bfloat16

END_TO_MID = [(0, 1), (3, 2)]
MID_TO_MID = [(1, 2), (2, 1)]
MID_TO_END = [(1, 0), (2, 3)]
RELATIVE = (0, 2, 1, 3)
OTHER_CORE = [(0, 1), (1, 0), (2, 3), (3, 2)]
OTHER_Y = [(0, 2), (2, 0), (1, 3), (3, 1)]
OTHER_OCC = [(0, 1), (1, 0)]
NEIGHBOUR = [(0, 1), (1, 0), (2, 3), (3, 2)]
ROOM = 60 << 20
CHEAP = pl.CostEstimate(flops=1 << 20, bytes_accessed=1 << 16, transcendentals=0)


def after(value, *earlier):
    return lax.optimization_barrier((value, *earlier))[0]


def dot_rows(lhs, rhs):
    return jnp.dot(lhs.reshape(-1, lhs.shape[-1]), rhs, preferred_element_type=F32)


def operands(products, first):
    specs, arrays, places = [], [], {}
    for place, (irrep, lhs, _) in enumerate(products):
        rows, depth = lhs.shape[-2] // 4, lhs.shape[-1]

        def quarter(p, r, where, place=place):
            return where[first + jnp.where(p == place, r, jnp.where(p < place, 0, 1))]
        if lhs.ndim == 4:
            specs.append(pl.BlockSpec(
                (1, 2, rows, depth), lambda p, r, where, g=irrep, q=quarter: (g, 0, q(p, r, where), 0)))
        else:
            specs.append(pl.BlockSpec((2, rows, depth), lambda p, r, where, q=quarter: (0, q(p, r, where), 0)))
        arrays.append(lhs)
    for _, _, rhs in products:
        if id(rhs) not in places:
            places[id(rhs)] = len(arrays)
            specs.append(pl.BlockSpec(rhs.shape, lambda p, r, where: (0, 0)))
            arrays.append(rhs)
    return specs, arrays, [places[id(rhs)] for _, _, rhs in products]


def run_products(refs, columns_at, use):
    for place, at in enumerate(columns_at):
        @pl.when(pl.program_id(0) == place)
        def _():
            use(dot_rows(refs[place][...], refs[at][...]))


def send_products(where, products):
    specs, arrays, columns_at = operands(products, 2)
    count, rows, columns = len(products), products[0][1].shape[-2] // 2, products[0][2].shape[1]

    def kernel(where_ref, *refs):
        def use(value):
            refs[-1][0, 0] = value.astype(BF16)
        run_products(refs, columns_at, use)

    return pl.pallas_call(
        kernel,
        out_shape=jax.ShapeDtypeStruct((count, 2, rows, columns), BF16),
        grid_spec=pltpu.PrefetchScalarGridSpec(
            num_scalar_prefetch=1,
            grid=(count, 2),
            in_specs=specs,
            out_specs=pl.BlockSpec((1, 1, rows, columns), lambda p, r, where: (p, r, 0, 0)),
        ),
        compiler_params=pltpu.CompilerParams(vmem_limit_bytes=ROOM),
        cost_estimate=CHEAP,
        name="send_products",
    )(where, *arrays)


def keep_products(where, products, arrived):
    specs, arrays, columns_at = operands(products, 0)
    count, rows, columns = len(products), products[0][1].shape[-2] // 2, products[0][2].shape[1]

    def kernel(where_ref, *refs):
        arrived_ref, away, own = refs[-3:]
        quarter = pl.program_id(1)

        def use(value):
            total = (value + arrived_ref[0, 0].astype(F32)).astype(BF16)

            @pl.when(quarter == 0)
            def _():
                own[0] = total

            @pl.when(quarter == 1)
            def _():
                away[0] = total
        run_products(refs, columns_at, use)

    return pl.pallas_call(
        kernel,
        out_shape=(jax.ShapeDtypeStruct((count, rows, columns), BF16),) * 2,
        grid_spec=pltpu.PrefetchScalarGridSpec(
            num_scalar_prefetch=1,
            grid=(count, 2),
            in_specs=specs + [pl.BlockSpec((1, 1, rows, columns), lambda p, r, where: (p, r, 0, 0))],
            out_specs=(pl.BlockSpec((1, rows, columns), lambda p, r, where: (p, 0, 0)),) * 2,
        ),
        compiler_params=pltpu.CompilerParams(vmem_limit_bytes=ROOM),
        cost_estimate=CHEAP,
        name="keep_products",
    )(where, *arrays, arrived)


def place(base, parity, kept, arrived, out, shape):
    count = len(kept)
    rows, columns = shape[2], shape[4]
    block = rows // 2

    def kernel(base_ref, *refs):
        out_ref, wide = refs[-2:]
        first = base_ref[1] == 0
        for index in range(count):
            mine, theirs = refs[index][0].astype(F32), refs[count + index][0].astype(F32)
            wide[:, index, :] = jnp.where(first, mine, theirs)
            wide[:, count + index, :] = jnp.where(first, theirs, mine)
        out_ref[0, 0] = wide[...].astype(BF16)

    pieces = kept + arrived
    specs = [
        pl.BlockSpec((1, block, columns), lambda a, i, base, j=j, step=array.shape[0] - 2: (
            a + step * (1 - base[1]), i, j))
        for array, j in pieces]
    extra = [] if out is None else [out]
    return pl.pallas_call(
        kernel,
        out_shape=jax.ShapeDtypeStruct(shape, BF16),
        grid_spec=pltpu.PrefetchScalarGridSpec(
            num_scalar_prefetch=1,
            grid=(2, rows // block),
            in_specs=specs + [pl.BlockSpec(memory_space=pl.ANY)] * len(extra),
            out_specs=pl.BlockSpec(
                (1, 1, block, 2 * count, columns),
                lambda a, i, base: (base[0] + (a + parity) % 2, a, i, 0, 0)),
            scratch_shapes=[pltpu.VMEM((block, 2 * count, columns), F32)],
        ),
        input_output_aliases={1 + 2 * count: 0} if extra else {},
        compiler_params=pltpu.CompilerParams(vmem_limit_bytes=ROOM),
        cost_estimate=CHEAP,
        name="place",
    )(base, *[array for array, _ in pieces], *extra)


class Order:
    def __init__(self):
        self.before, self.edge = [], []

    def follow(self, value):
        return after(value, *self.before) if self.before else value

    def step(self, value):
        self.before = [value]
        return value

    def phase(self, *values):
        self.before = self.before + list(values)
        self.edge = self.before

    def open(self, value):
        return after(value, *self.edge) if self.edge else value


class Batch:
    def __init__(self, order, where, *products):
        self.order, self.where, self.products = order, where, products

    def send(self):
        followed = {id(rhs): rhs for _, _, rhs in self.products}
        followed = {key: self.order.follow(rhs) for key, rhs in followed.items()}
        self.products = [(irrep, lhs, followed[id(rhs)]) for irrep, lhs, rhs in self.products]
        part = self.order.step(send_products(self.where, self.products))
        self.arrived = lax.ppermute(part, "ka", OTHER_CORE)

    def keep(self):
        arrived = self.order.follow(self.arrived)
        self.away, self.own = keep_products(self.where, self.products, arrived)
        self.order.step(self.away)

    def swap(self):
        self.other = lax.ppermute(self.order.open(self.away), "ka", OTHER_Y)

    def finish(self):
        other = self.order.follow(self.other)
        total = self.order.step((self.own.astype(F32) + other.astype(F32)).astype(BF16))
        count, rows, columns = total.shape
        return [total[p].reshape(2, rows // 2, columns) for p in range(count)]


def line_local(ladder_amplitudes, ladder_integrals, cycle_amplitudes, cycle_integrals):
    vir, occ, ka = (lax.axis_index(name) for name in ("vir", "occ", "ka"))
    irreps, rows_here, group, depth = cycle_amplitudes.shape
    quarter = group // 4
    columns = cycle_integrals.shape[3]
    at_end = (vir == 0) | (vir == 3)
    where = jnp.bitwise_xor(ka, jnp.array(RELATIVE, jnp.int32))
    order = Order()

    def columns_of(g):
        return order.open(cycle_integrals)[g].reshape(depth, 2 * columns)

    def batch(*products):
        return Batch(order, where, *products)

    def move(value, route):
        return lax.ppermute(order.open(value), "vir", route)

    def cross(near, far):
        near, far = order.open(near), order.open(far)
        away = jnp.where(occ == 0, far, near)
        return jnp.where(occ == 0, near, far), lax.ppermute(away, "occ", OTHER_OCC)

    def home(mine, back):
        return jnp.where(at_end, order.open(back), order.open(mine))

    low = jnp.where((occ == 0) | at_end, 0, 2).astype(jnp.int32)
    shape = (8 // 2, rows_here, quarter, 2 * irreps, columns)

    def put(half, j, crossed, out):
        base = jnp.stack([low if half == 0 else 2 - low, occ.astype(jnp.int32)])
        kept = [(pair[0], jj) for pair, jj in crossed]
        arrived = [(pair[1], jj) for pair, jj in crossed]
        return order.step(place(base, j, kept, arrived, out, shape))

    def rows_of(g):
        return order.open(cycle_amplitudes)[g]

    def straight(near, near_in, rows, one=slice(None)):
        own_rows, foreign = (order.open(value) for value in rows)
        first = lax.ppermute(jnp.where(occ == 0, own_rows, foreign), ("vir", "occ"), [(2, 3), (4, 5), (3, 1), (5, 7)])
        second = lax.ppermute(foreign, ("vir", "occ"), [(2, 1), (4, 7)])
        kept = jnp.where(occ == 0, near[..., one], jnp.where(at_end, first, own_rows))
        arrived = jnp.where(occ == 0, near_in[..., one], jnp.where(at_end, second, first))
        return kept, arrived

    def over(near):
        return lax.ppermute(order.open(near), "occ", [(1, 0)])

    ca = cycle_amplitudes
    b0 = columns_of(0)
    order.phase(b0)
    own0 = move(b0, MID_TO_MID)
    a0 = move(rows_of(0), END_TO_MID)
    b3, b1 = columns_of(3), columns_of(1)
    one = batch((3, ca, b3), (1, ca, b1))
    one.send()
    one.keep()

    order.phase(own0, a0)
    own3 = move(b3, MID_TO_MID)
    swap3 = move(b3, NEIGHBOUR)
    one.swap()
    two = batch((0, ca, own0), (0, a0, own0))
    two.send()
    two.keep()
    s3, s1 = one.finish()

    order.phase(own3, swap3)
    relay3 = move(swap3, MID_TO_MID)
    b0_in = move(b0, END_TO_MID)
    on3 = move(own3, MID_TO_END)
    two.swap()
    b2 = columns_of(2)
    three = batch((3, ca, swap3), (0, ca, b0), (0, a0, b0))
    three.send()
    three.keep()
    f0 = two.finish()

    order.phase(relay3, b0_in, on3)
    relay0 = move(b0_in, MID_TO_MID)
    a1 = move(rows_of(1), END_TO_MID)
    on_relay3 = move(relay3, MID_TO_END)
    three.swap()
    four = batch((2, ca, b2), (0, ca, b0_in), (3, ca, jnp.where(at_end, order.open(on3), own3)))
    four.send()
    four.keep()
    n3, *s0 = three.finish()

    order.phase(relay0, a1, on_relay3)
    own1 = move(b1, MID_TO_MID)
    a2 = move(rows_of(2), END_TO_MID)
    f0_back = move(f0[1], MID_TO_END)
    s0_back = move(s0[1], MID_TO_END)
    four.swap()
    five = batch((0, ca, relay0), (0, a0, relay0), (3, ca, jnp.where(at_end, order.open(on_relay3), relay3)))
    five.send()
    five.keep()
    s2, n0, f3 = four.finish()

    order.phase(own1, a2, f0_back, s0_back)
    own2 = move(b2, MID_TO_MID)
    swap1 = move(b1, NEIGHBOUR)
    x0a = cross(s0[0], home(f0[0], f0_back))
    five.swap()
    six = batch((1, ca, own1), (1, a1, own1))
    six.send()
    six.keep()
    *g0, g3 = five.finish()

    order.phase(own2, swap1, x0a[1])
    relay1 = move(swap1, MID_TO_MID)
    swap2 = move(b2, NEIGHBOUR)
    gathered = lax.all_gather(order.open(ladder_amplitudes), "vir", axis=0, tiled=True)
    x3a = cross(s3, f3)
    six.swap()
    seven = batch((2, ca, own2), (2, a2, own2), (1, ca, swap1))
    seven.send()
    seven.keep()
    f1 = six.finish()

    order.phase(relay1, swap2, x3a[1])
    relay2 = [move(swap2[:, :columns], MID_TO_MID)]
    g0_back = move(g0[1], MID_TO_END)
    f1_back = move(f1[1], MID_TO_END)
    x3b = cross(n3, g3)
    seven.swap()
    eight = batch((1, ca, relay1), (1, a1, relay1), (2, ca, swap2))
    eight.send()
    eight.keep()
    *f2, n1 = seven.finish()

    order.phase(relay2[0], g0_back, f1_back, x3b[1])
    relay2.append(move(swap2[:, columns:], MID_TO_MID))
    f2_back = move(f2[1], MID_TO_END)
    x0b = cross(home(n0, s0_back), home(g0[0], g0_back))
    x1a = cross(s1, home(f1[0], f1_back))
    near1_in = over(n1)
    eight.swap()
    nine = batch((2, ca, relay2[0]), (2, a2, relay2[0]))
    nine.send()
    nine.keep()
    *g1, n2 = eight.finish()

    order.phase(relay2[1], f2_back, x0b[1], x1a[1], near1_in, gathered)
    near2_in = over(n2)
    x2a = cross(s2, home(f2[0], f2_back))
    nine.swap()
    ten = batch((2, ca, relay2[1]), (2, a2, relay2[1]))
    ten.send()
    ten.keep()
    ten.swap()
    x1b = straight(n1, near1_in, g1)
    x2b = [straight(n2, near2_in, nine.finish(), slice(0, columns))]
    partial_ladder = order.step(jnp.dot(
        order.follow(gathered), ladder_integrals, preferred_element_type=F32,
    ).astype(BF16))
    ladder_residual = lax.psum_scatter(partial_ladder, ("occ", "ka"), scatter_dimension=0, tiled=True)
    x2b.append(straight(n2, near2_in, ten.finish(), slice(columns, 2 * columns)))
    out = None
    for j in range(2):
        out = put(0, j, [(x0a, j), (x1a, j), (x2a, j), (x3a, j)], out)
    for j in range(2):
        out = put(1, j, [(x0b, j), (x1b, j), (x2b[j], 0), (x3b, j)], out)
    return ladder_residual, out


def regroup(blocks):
    local_rows = blocks.shape[1]
    first_irrep = lax.axis_index("vir") * local_rows
    pieces = []
    for local_index in range(local_rows):
        permuted = jnp.bitwise_xor(first_irrep + local_index, jnp.arange(8, dtype=jnp.int32))
        pieces.append(jnp.take(blocks[:, local_index], permuted, axis=2))
    stacked = jnp.stack(pieces, axis=1)
    return jnp.transpose(stacked, (3, 1, 2, 0, 4))


def any_local(ladder_amplitudes, ladder_integrals, cycle_amplitudes, cycle_integrals):
    partial_ladder = jnp.dot(
        lax.all_gather(ladder_amplitudes, "vir", axis=0, tiled=True),
        ladder_integrals,
        preferred_element_type=F32,
    )
    summed_ladder = lax.psum_scatter(
        partial_ladder.astype(BF16), ("occ", "ka"), scatter_dimension=0, tiled=True
    )
    partial_cycle = jnp.einsum(
        "gaxk,gkny->gaxny",
        cycle_amplitudes,
        lax.all_gather(cycle_integrals, "vir", axis=2, tiled=True),
        preferred_element_type=F32,
    )
    summed_cycle = lax.psum_scatter(
        partial_cycle.astype(BF16), "ka", scatter_dimension=2, tiled=True
    )
    arranged = regroup(summed_cycle)
    cycle_residual = lax.all_to_all(arranged, "occ", split_axis=0, concat_axis=3, tiled=True)
    return (summed_ladder, cycle_residual)


def solution(mesh):
    line = (mesh.shape["vir"], mesh.shape["occ"], mesh.shape["ka"]) == (4, 2, 4)
    placed = (
        P("vir", ("occ", "ka")),
        P(("occ", "ka"), "vir"),
        P("occ", "vir", None, "ka"),
        P("occ", "ka", "vir", None),
    )
    return jax.shard_map(
        line_local if line else any_local,
        mesh=mesh,
        in_specs=placed,
        out_specs=(P(("occ", "ka"), "vir"), P("occ", "vir", "ka", None, None)),
        check_vma=False,
    )
```

```python
import jax
import jax.numpy as jnp
from jax import lax
from jax.experimental import pallas as pl
from jax.experimental.pallas import tpu as pltpu
from jax.sharding import PartitionSpec as P

F32, BF16 = jnp.float32, jnp.bfloat16

END_TO_MID = [(0, 1), (3, 2)]
MID_TO_MID = [(1, 2), (2, 1)]
MID_TO_END = [(1, 0), (2, 3)]
RELATIVE = (0, 2, 1, 3)
OTHER_CORE = [(0, 1), (1, 0), (2, 3), (3, 2)]
OTHER_Y = [(0, 2), (2, 0), (1, 3), (3, 1)]
OTHER_OCC = [(0, 1), (1, 0)]
NEIGHBOUR = [(0, 1), (1, 0), (2, 3), (3, 2)]
ROOM = 60 << 20
CHEAP = pl.CostEstimate(flops=1 << 20, bytes_accessed=1 << 16, transcendentals=0)


def after(value, *earlier):
    return lax.optimization_barrier((value, *earlier))[0]


def dot_rows(lhs, rhs):
    return jnp.dot(lhs.reshape(-1, lhs.shape[-1]), rhs, preferred_element_type=F32)


def operands(products, first):
    specs, arrays, places = [], [], {}
    for place, (irrep, lhs, _) in enumerate(products):
        rows, depth = lhs.shape[-2] // 4, lhs.shape[-1]

        def quarter(p, r, where, place=place):
            return where[first + jnp.where(p == place, r, jnp.where(p < place, 0, 1))]
        if lhs.ndim == 4:
            specs.append(pl.BlockSpec(
                (1, 2, rows, depth), lambda p, r, where, g=irrep, q=quarter: (g, 0, q(p, r, where), 0)))
        else:
            specs.append(pl.BlockSpec((2, rows, depth), lambda p, r, where, q=quarter: (0, q(p, r, where), 0)))
        arrays.append(lhs)
    for _, _, rhs in products:
        if id(rhs) not in places:
            places[id(rhs)] = len(arrays)
            specs.append(pl.BlockSpec(rhs.shape, lambda p, r, where: (0, 0)))
            arrays.append(rhs)
    return specs, arrays, [places[id(rhs)] for _, _, rhs in products]


def run_products(refs, columns_at, use):
    for place, at in enumerate(columns_at):
        @pl.when(pl.program_id(0) == place)
        def _():
            use(dot_rows(refs[place][...], refs[at][...]))


def send_products(where, products):
    specs, arrays, columns_at = operands(products, 2)
    count, rows, columns = len(products), products[0][1].shape[-2] // 2, products[0][2].shape[1]

    def kernel(where_ref, *refs):
        def use(value):
            for quarter, out in enumerate(refs[-2:]):
                @pl.when(pl.program_id(1) == quarter)
                def _():
                    out[0] = value.astype(BF16)
        run_products(refs, columns_at, use)

    return pl.pallas_call(
        kernel,
        out_shape=(jax.ShapeDtypeStruct((count, rows, columns), BF16),) * 2,
        grid_spec=pltpu.PrefetchScalarGridSpec(
            num_scalar_prefetch=1,
            grid=(count, 2),
            in_specs=specs,
            out_specs=(pl.BlockSpec((1, rows, columns), lambda p, r, where: (p, 0, 0)),) * 2,
        ),
        compiler_params=pltpu.CompilerParams(vmem_limit_bytes=ROOM),
        cost_estimate=CHEAP,
        name="send_products",
    )(where, *arrays)


def keep_products(where, products, arrived):
    specs, arrays, columns_at = operands(products, 0)
    count, rows, columns = len(products), products[0][1].shape[-2] // 2, products[0][2].shape[1]

    def kernel(where_ref, *refs):
        def use(value):
            for quarter, (arrived_ref, out) in enumerate(zip(refs[-4:-2], refs[-2:])):
                @pl.when(pl.program_id(1) == quarter)
                def _():
                    out[0] = (value + arrived_ref[0].astype(F32)).astype(BF16)
        run_products(refs, columns_at, use)

    return pl.pallas_call(
        kernel,
        out_shape=(jax.ShapeDtypeStruct((count, rows, columns), BF16),) * 2,
        grid_spec=pltpu.PrefetchScalarGridSpec(
            num_scalar_prefetch=1,
            grid=(count, 2),
            in_specs=specs + [pl.BlockSpec((1, rows, columns), lambda p, r, where: (p, 0, 0))] * 2,
            out_specs=(pl.BlockSpec((1, rows, columns), lambda p, r, where: (p, 0, 0)),) * 2,
        ),
        compiler_params=pltpu.CompilerParams(vmem_limit_bytes=ROOM),
        cost_estimate=CHEAP,
        name="keep_products",
    )(where, *arrays, *arrived)


def place(base, parity, kept, arrived, out, shape):
    count = len(kept)
    rows, columns = shape[2], shape[4]
    block = rows // 2

    def kernel(base_ref, *refs):
        out_ref, wide = refs[-2:]
        first = base_ref[1] == 0
        for index in range(count):
            mine, theirs = refs[index][0].astype(F32), refs[count + index][0].astype(F32)
            wide[:, index, :] = jnp.where(first, mine, theirs)
            wide[:, count + index, :] = jnp.where(first, theirs, mine)
        out_ref[0, 0] = wide[...].astype(BF16)

    pieces = kept + arrived
    specs = [
        pl.BlockSpec((1, block, columns), lambda a, i, base, j=j, step=array.shape[0] - 2: (
            a + step * (1 - base[1]), i, j))
        for array, j in pieces]
    extra = [] if out is None else [out]
    return pl.pallas_call(
        kernel,
        out_shape=jax.ShapeDtypeStruct(shape, BF16),
        grid_spec=pltpu.PrefetchScalarGridSpec(
            num_scalar_prefetch=1,
            grid=(2, rows // block),
            in_specs=specs + [pl.BlockSpec(memory_space=pl.ANY)] * len(extra),
            out_specs=pl.BlockSpec(
                (1, 1, block, 2 * count, columns),
                lambda a, i, base: (base[0] + (a + parity) % 2, a, i, 0, 0)),
            scratch_shapes=[pltpu.VMEM((block, 2 * count, columns), F32)],
        ),
        input_output_aliases={1 + 2 * count: 0} if extra else {},
        compiler_params=pltpu.CompilerParams(vmem_limit_bytes=ROOM),
        cost_estimate=CHEAP,
        name="place",
    )(base, *[array for array, _ in pieces], *extra)


class Order:
    def __init__(self):
        self.before, self.edge = [], []

    def follow(self, value):
        return after(value, *self.before) if self.before else value

    def step(self, value):
        self.before = [value]
        return value

    def phase(self, *values):
        self.before = self.before + list(values)
        self.edge = self.before

    def open(self, value):
        return after(value, *self.edge) if self.edge else value


class Batch:
    def __init__(self, order, where, *products):
        self.order, self.where, self.products = order, where, products

    def send(self):
        followed = {id(rhs): rhs for _, _, rhs in self.products}
        followed = {key: self.order.follow(rhs) for key, rhs in followed.items()}
        self.products = [(irrep, lhs, followed[id(rhs)]) for irrep, lhs, rhs in self.products]
        parts = send_products(self.where, self.products)
        self.order.step(parts[1])
        self.arrived = [lax.ppermute(part, "ka", OTHER_CORE) for part in parts]

    def keep(self):
        arrived = [self.order.follow(part) for part in self.arrived]
        self.own, self.away = keep_products(self.where, self.products, arrived)
        self.order.step(self.away)

    def swap(self):
        self.other = lax.ppermute(self.order.open(self.away), "ka", OTHER_Y)

    def finish(self):
        other = self.order.follow(self.other)
        total = self.order.step((self.own.astype(F32) + other.astype(F32)).astype(BF16))
        count, rows, columns = total.shape
        return [total[p].reshape(2, rows // 2, columns) for p in range(count)]


def line_local(ladder_amplitudes, ladder_integrals, cycle_amplitudes, cycle_integrals):
    vir, occ, ka = (lax.axis_index(name) for name in ("vir", "occ", "ka"))
    irreps, rows_here, group, depth = cycle_amplitudes.shape
    quarter = group // 4
    columns = cycle_integrals.shape[3]
    at_end = (vir == 0) | (vir == 3)
    where = jnp.bitwise_xor(ka, jnp.array(RELATIVE, jnp.int32))
    order = Order()

    def columns_of(g):
        return order.open(cycle_integrals)[g].reshape(depth, 2 * columns)

    def exchange(inwards, outwards):
        return move(jnp.where(at_end, order.open(inwards), order.open(outwards)), NEIGHBOUR)

    def batch(*products):
        return Batch(order, where, *products)

    def move(value, route):
        return lax.ppermute(order.open(value), "vir", route)

    def cross(near, far):
        near, far = order.open(near), order.open(far)
        away = jnp.where(occ == 0, far, near)
        return jnp.where(occ == 0, near, far), lax.ppermute(away, "occ", OTHER_OCC)

    def home(mine, back):
        return jnp.where(at_end, order.open(back), order.open(mine))

    low = jnp.where((occ == 0) | at_end, 0, 2).astype(jnp.int32)
    shape = (8 // 2, rows_here, quarter, 2 * irreps, columns)

    def put(half, j, crossed, out):
        base = jnp.stack([low if half == 0 else 2 - low, occ.astype(jnp.int32)])
        kept = [(pair[0], jj) for pair, jj in crossed]
        arrived = [(pair[1], jj) for pair, jj in crossed]
        return order.step(place(base, j, kept, arrived, out, shape))

    def rows_of(g):
        return order.open(cycle_amplitudes)[g]

    def straight(near, near_in, rows, one=slice(None)):
        own_rows, foreign = (order.open(value) for value in rows)
        first = lax.ppermute(jnp.where(occ == 0, own_rows, foreign), ("vir", "occ"), [(2, 3), (4, 5), (3, 1), (5, 7)])
        second = lax.ppermute(foreign, ("vir", "occ"), [(2, 1), (4, 7)])
        kept = jnp.where(occ == 0, near[..., one], jnp.where(at_end, first, own_rows))
        arrived = jnp.where(occ == 0, near_in[..., one], jnp.where(at_end, second, first))
        return kept, arrived

    def over(near):
        return lax.ppermute(order.open(near), "occ", [(1, 0)])

    ca = cycle_amplitudes
    b0 = columns_of(0)
    order.phase(b0)
    own0 = move(b0, MID_TO_MID)
    a0 = move(rows_of(0), END_TO_MID)
    b3, b1 = columns_of(3), columns_of(1)
    one = batch((3, ca, b3), (1, ca, b1))
    one.send()
    one.keep()

    order.phase(own0, a0)
    own3 = move(b3, MID_TO_MID)
    swap3 = move(b3, NEIGHBOUR)
    one.swap()
    two = batch((0, ca, own0), (0, a0, own0))
    two.send()
    two.keep()
    s3, s1 = one.finish()

    order.phase(own3, swap3)
    relay3 = move(swap3, MID_TO_MID)
    both3 = exchange(b0, own3)
    two.swap()
    b2 = columns_of(2)
    three = batch((3, ca, swap3), (0, ca, b0), (0, a0, b0))
    three.send()
    three.keep()
    f0 = two.finish()

    order.phase(relay3, both3)
    relay0 = move(both3, MID_TO_MID)
    both4 = exchange(rows_of(1).reshape(b0.shape), relay3)
    three.swap()
    four = batch((2, ca, b2), (0, ca, both3), (3, ca, jnp.where(at_end, order.open(both3), own3)))
    four.send()
    four.keep()
    n3, *s0 = three.finish()
    rows2 = rows_of(2)

    order.phase(relay0, both4, rows2)
    a1 = both4.reshape(a0.shape)
    own1 = move(b1, MID_TO_MID)
    a2 = move(rows2, END_TO_MID)
    backs = move(jnp.stack([f0[1], s0[1]]), MID_TO_END)
    four.swap()
    five = batch((0, ca, relay0), (0, a0, relay0), (3, ca, jnp.where(at_end, order.open(both4), relay3)))
    five.send()
    five.keep()
    s2, n0, f3 = four.finish()

    order.phase(own1, a2, backs)
    f0_back, s0_back = backs[0], backs[1]
    own2 = move(b2, MID_TO_MID)
    swap1 = move(b1, NEIGHBOUR)
    x0a = cross(s0[0], home(f0[0], f0_back))
    five.swap()
    six = batch((1, ca, own1), (1, a1, own1))
    six.send()
    six.keep()
    *g0, g3 = five.finish()

    order.phase(own2, swap1, x0a[1])
    relay1 = move(swap1, MID_TO_MID)
    swap2 = move(b2, NEIGHBOUR)
    x3a = cross(s3, f3)
    six.swap()
    seven = batch((2, ca, own2), (2, a2, own2), (1, ca, swap1))
    seven.send()
    seven.keep()
    f1 = six.finish()

    order.phase(relay1, swap2, x3a[1])
    gathered = lax.all_gather(order.open(ladder_amplitudes), "vir", axis=0, tiled=True)
    relay2 = [move(swap2[:, :columns], MID_TO_MID)]
    g0_back = move(g0[1], MID_TO_END)
    f1_back = move(f1[1], MID_TO_END)
    x3b = cross(n3, g3)
    seven.swap()
    eight = batch((1, ca, relay1), (1, a1, relay1), (2, ca, swap2))
    eight.send()
    eight.keep()
    *f2, n1 = seven.finish()

    order.phase(relay2[0], g0_back, f1_back, x3b[1])
    relay2.append(move(swap2[:, columns:], MID_TO_MID))
    f2_back = move(f2[1], MID_TO_END)
    x0b = cross(home(n0, s0_back), home(g0[0], g0_back))
    x1a = cross(s1, home(f1[0], f1_back))
    near1_in = over(n1)
    eight.swap()
    nine = batch((2, ca, relay2[0]), (2, a2, relay2[0]))
    nine.send()
    nine.keep()
    *g1, n2 = eight.finish()

    order.phase(relay2[1], f2_back, x0b[1], x1a[1], near1_in, gathered)
    partial_ladder = order.step(jnp.dot(
        order.follow(gathered), ladder_integrals, preferred_element_type=F32,
    ).astype(BF16))
    ladder_residual = lax.psum_scatter(partial_ladder, ("occ", "ka"), scatter_dimension=0, tiled=True)
    near2_in = over(n2)
    x2a = cross(s2, home(f2[0], f2_back))
    nine.swap()
    ten = batch((2, ca, relay2[1]), (2, a2, relay2[1]))
    ten.send()
    ten.keep()
    ten.swap()
    x1b = straight(n1, near1_in, g1)
    x2b = [straight(n2, near2_in, nine.finish(), slice(0, columns))]
    x2b.append(straight(n2, near2_in, ten.finish(), slice(columns, 2 * columns)))
    out = None
    for j in range(2):
        out = put(0, j, [(x0a, j), (x1a, j), (x2a, j), (x3a, j)], out)
    for j in range(2):
        out = put(1, j, [(x0b, j), (x1b, j), (x2b[j], 0), (x3b, j)], out)
    return ladder_residual, out


def regroup(blocks):
    local_rows = blocks.shape[1]
    first_irrep = lax.axis_index("vir") * local_rows
    pieces = []
    for local_index in range(local_rows):
        permuted = jnp.bitwise_xor(first_irrep + local_index, jnp.arange(8, dtype=jnp.int32))
        pieces.append(jnp.take(blocks[:, local_index], permuted, axis=2))
    stacked = jnp.stack(pieces, axis=1)
    return jnp.transpose(stacked, (3, 1, 2, 0, 4))


def any_local(ladder_amplitudes, ladder_integrals, cycle_amplitudes, cycle_integrals):
    partial_ladder = jnp.dot(
        lax.all_gather(ladder_amplitudes, "vir", axis=0, tiled=True),
        ladder_integrals,
        preferred_element_type=F32,
    )
    summed_ladder = lax.psum_scatter(
        partial_ladder.astype(BF16), ("occ", "ka"), scatter_dimension=0, tiled=True
    )
    partial_cycle = jnp.einsum(
        "gaxk,gkny->gaxny",
        cycle_amplitudes,
        lax.all_gather(cycle_integrals, "vir", axis=2, tiled=True),
        preferred_element_type=F32,
    )
    summed_cycle = lax.psum_scatter(
        partial_cycle.astype(BF16), "ka", scatter_dimension=2, tiled=True
    )
    arranged = regroup(summed_cycle)
    cycle_residual = lax.all_to_all(arranged, "occ", split_axis=0, concat_axis=3, tiled=True)
    return (summed_ladder, cycle_residual)


def solution(mesh):
    line = (mesh.shape["vir"], mesh.shape["occ"], mesh.shape["ka"]) == (4, 2, 4)
    placed = (
        P("vir", ("occ", "ka")),
        P(("occ", "ka"), "vir"),
        P("occ", "vir", None, "ka"),
        P("occ", "ka", "vir", None),
    )
    return jax.shard_map(
        line_local if line else any_local,
        mesh=mesh,
        in_specs=placed,
        out_specs=(P(("occ", "ka"), "vir"), P("occ", "vir", "ka", None, None)),
        check_vma=False,
    )
```

```python
import jax
import jax.numpy as jnp
from jax import lax
from jax.experimental import pallas as pl
from jax.experimental.pallas import tpu as pltpu
from jax.sharding import PartitionSpec as P

F32, BF16 = jnp.float32, jnp.bfloat16

END_TO_MID = [(0, 1), (3, 2)]
MID_TO_MID = [(1, 2), (2, 1)]
MID_TO_END = [(1, 0), (2, 3)]
RELATIVE = (0, 2, 1, 3)
OTHER_CORE = [(0, 1), (1, 0), (2, 3), (3, 2)]
OTHER_Y = [(0, 2), (2, 0), (1, 3), (3, 1)]
OTHER_OCC = [(0, 1), (1, 0)]
NEIGHBOUR = [(0, 1), (1, 0), (2, 3), (3, 2)]
ROOM = 60 << 20
CHEAP = pl.CostEstimate(flops=1 << 20, bytes_accessed=1 << 16, transcendentals=0)


def after(value, *earlier):
    return lax.optimization_barrier((value, *earlier))[0]


def dot_rows(lhs, rhs):
    return jnp.dot(lhs.reshape(-1, lhs.shape[-1]), rhs, preferred_element_type=F32)


def operands(products, first):
    specs, arrays, places = [], [], {}
    for place, (irrep, lhs, _) in enumerate(products):
        rows, depth = lhs.shape[-2] // 4, lhs.shape[-1]

        def quarter(p, r, where, place=place):
            return where[first + jnp.where(p == place, r, jnp.where(p < place, 0, 1))]
        if lhs.ndim == 4:
            specs.append(pl.BlockSpec(
                (1, 2, rows, depth), lambda p, r, where, g=irrep, q=quarter: (g, 0, q(p, r, where), 0)))
        else:
            specs.append(pl.BlockSpec((2, rows, depth), lambda p, r, where, q=quarter: (0, q(p, r, where), 0)))
        arrays.append(lhs)
    for _, _, rhs in products:
        if id(rhs) not in places:
            places[id(rhs)] = len(arrays)
            specs.append(pl.BlockSpec(rhs.shape, lambda p, r, where: (0, 0)))
            arrays.append(rhs)
    return specs, arrays, [places[id(rhs)] for _, _, rhs in products]


def run_products(refs, columns_at, use):
    for place, at in enumerate(columns_at):
        @pl.when(pl.program_id(0) == place)
        def _():
            use(dot_rows(refs[place][...], refs[at][...]))


def send_products(where, products):
    specs, arrays, columns_at = operands(products, 2)
    count, rows, columns = len(products), products[0][1].shape[-2] // 2, products[0][2].shape[1]

    def kernel(where_ref, *refs):
        def use(value):
            for quarter, out in enumerate(refs[-2:]):
                @pl.when(pl.program_id(1) == quarter)
                def _():
                    out[0] = value.astype(BF16)
        run_products(refs, columns_at, use)

    return pl.pallas_call(
        kernel,
        out_shape=(jax.ShapeDtypeStruct((count, rows, columns), BF16),) * 2,
        grid_spec=pltpu.PrefetchScalarGridSpec(
            num_scalar_prefetch=1,
            grid=(count, 2),
            in_specs=specs,
            out_specs=(pl.BlockSpec((1, rows, columns), lambda p, r, where: (p, 0, 0)),) * 2,
        ),
        compiler_params=pltpu.CompilerParams(vmem_limit_bytes=ROOM),
        cost_estimate=CHEAP,
        name="send_products",
    )(where, *arrays)


def keep_products(where, products, arrived):
    specs, arrays, columns_at = operands(products, 0)
    count, rows, columns = len(products), products[0][1].shape[-2] // 2, products[0][2].shape[1]

    def kernel(where_ref, *refs):
        def use(value):
            for quarter, (arrived_ref, out) in enumerate(zip(refs[-4:-2], refs[-2:])):
                @pl.when(pl.program_id(1) == quarter)
                def _():
                    out[0] = (value + arrived_ref[0].astype(F32)).astype(BF16)
        run_products(refs, columns_at, use)

    return pl.pallas_call(
        kernel,
        out_shape=(jax.ShapeDtypeStruct((count, rows, columns), BF16),) * 2,
        grid_spec=pltpu.PrefetchScalarGridSpec(
            num_scalar_prefetch=1,
            grid=(count, 2),
            in_specs=specs + [pl.BlockSpec((1, rows, columns), lambda p, r, where: (p, 0, 0))] * 2,
            out_specs=(pl.BlockSpec((1, rows, columns), lambda p, r, where: (p, 0, 0)),) * 2,
        ),
        compiler_params=pltpu.CompilerParams(vmem_limit_bytes=ROOM),
        cost_estimate=CHEAP,
        name="keep_products",
    )(where, *arrays, *arrived)


def place(base, parity, kept, arrived, out, shape):
    count = len(kept)
    rows, columns = shape[2], shape[4]
    block = rows // 2

    def kernel(base_ref, *refs):
        out_ref, wide = refs[-2:]
        first = base_ref[1] == 0
        for index in range(count):
            mine, theirs = refs[index][0].astype(F32), refs[count + index][0].astype(F32)
            wide[:, index, :] = jnp.where(first, mine, theirs)
            wide[:, count + index, :] = jnp.where(first, theirs, mine)
        out_ref[0, 0] = wide[...].astype(BF16)

    pieces = kept + arrived
    specs = [
        pl.BlockSpec((1, block, columns), lambda a, i, base, j=j, first=first: (first + a, i, j))
        for _, first, j in pieces]
    extra = [] if out is None else [out]
    return pl.pallas_call(
        kernel,
        out_shape=jax.ShapeDtypeStruct(shape, BF16),
        grid_spec=pltpu.PrefetchScalarGridSpec(
            num_scalar_prefetch=1,
            grid=(2, rows // block),
            in_specs=specs + [pl.BlockSpec(memory_space=pl.ANY)] * len(extra),
            out_specs=pl.BlockSpec(
                (1, 1, block, 2 * count, columns),
                lambda a, i, base: (base[0] + (a + parity) % 2, a, i, 0, 0)),
            scratch_shapes=[pltpu.VMEM((block, 2 * count, columns), F32)],
        ),
        input_output_aliases={1 + 2 * count: 0} if extra else {},
        compiler_params=pltpu.CompilerParams(vmem_limit_bytes=ROOM),
        cost_estimate=CHEAP,
        name="place",
    )(base, *[array for array, _, _ in pieces], *extra)


class Order:
    def __init__(self):
        self.before, self.edge = [], []

    def follow(self, value):
        return after(value, *self.before) if self.before else value

    def step(self, value):
        self.before = [value]
        return value

    def phase(self, *values):
        self.before = self.before + list(values)
        self.edge = self.before

    def open(self, value):
        return after(value, *self.edge) if self.edge else value


class Batch:
    def __init__(self, order, where, *products):
        self.order, self.where, self.products = order, where, products

    def send(self):
        followed = {id(rhs): rhs for _, _, rhs in self.products}
        followed = {key: self.order.follow(rhs) for key, rhs in followed.items()}
        self.products = [(irrep, lhs, followed[id(rhs)]) for irrep, lhs, rhs in self.products]
        parts = send_products(self.where, self.products)
        self.order.step(parts[1])
        self.arrived = [lax.ppermute(part, "ka", OTHER_CORE) for part in parts]

    def keep(self):
        arrived = [self.order.follow(part) for part in self.arrived]
        self.own, self.away = keep_products(self.where, self.products, arrived)
        self.order.step(self.away)

    def swap(self):
        self.other = lax.ppermute(self.order.open(self.away), "ka", OTHER_Y)

    def finish(self):
        total = (self.own.astype(F32) + self.order.open(self.other).astype(F32)).astype(BF16)
        count, rows, columns = total.shape
        return [total[p].reshape(2, rows // 2, columns) for p in range(count)]


def line_local(ladder_amplitudes, ladder_integrals, cycle_amplitudes, cycle_integrals):
    vir, occ, ka = (lax.axis_index(name) for name in ("vir", "occ", "ka"))
    irreps, rows_here, group, depth = cycle_amplitudes.shape
    quarter = group // 4
    columns = cycle_integrals.shape[3]
    at_end = (vir == 0) | (vir == 3)
    where = jnp.bitwise_xor(ka, jnp.array(RELATIVE, jnp.int32))
    order = Order()

    def columns_of(g):
        return order.open(cycle_integrals)[g].reshape(depth, 2 * columns)

    def exchange(inwards, outwards):
        return move(jnp.where(at_end, order.open(inwards), order.open(outwards)), NEIGHBOUR)

    def batch(*products):
        return Batch(order, where, *products)

    def move(value, route):
        return lax.ppermute(order.open(value), "vir", route)

    def cross(*pairs):
        pairs = [(order.open(near), order.open(far)) for near, far in pairs]
        away = jnp.concatenate([jnp.where(occ == 0, far, near) for near, far in pairs])
        return [jnp.where(occ == 0, near, far) for near, far in pairs], lax.ppermute(away, "occ", OTHER_OCC)

    def home(mine, back):
        return jnp.where(at_end, order.open(back), order.open(mine))

    low = jnp.where((occ == 0) | at_end, 0, 2).astype(jnp.int32)
    shape = (8 // 2, rows_here, quarter, 2 * irreps, columns)

    def put(half, j, crossed, out):
        base = jnp.stack([low if half == 0 else 2 - low, occ.astype(jnp.int32)])
        kept = [(pair[0][index], 0, jj) for pair, index, jj in crossed]
        arrived = [(pair[1], 2 * index, jj) for pair, index, jj in crossed]
        return order.step(place(base, j, kept, arrived, out, shape))

    def rows_of(g):
        return order.open(cycle_amplitudes)[g]

    def straight(near, near_in, rows, one=slice(None)):
        own_rows, foreign = (order.open(value) for value in rows)
        first = lax.ppermute(jnp.where(occ == 0, own_rows, foreign), ("vir", "occ"), [(2, 3), (4, 5), (3, 1), (5, 7)])
        second = lax.ppermute(foreign, ("vir", "occ"), [(2, 1), (4, 7)])
        kept = jnp.where(occ == 0, near[..., one], jnp.where(at_end, first, own_rows))
        arrived = jnp.where(occ == 0, near_in[..., one], jnp.where(at_end, second, first))
        return [kept], arrived

    def over(near):
        return lax.ppermute(order.open(near), "occ", [(1, 0)])

    ca = cycle_amplitudes
    b0 = columns_of(0)
    order.phase(b0)
    own0 = move(b0, MID_TO_MID)
    a0 = move(rows_of(0), END_TO_MID)
    b3, b1 = columns_of(3), columns_of(1)
    one = batch((3, ca, b3), (1, ca, b1))
    one.send()
    one.keep()

    order.phase(own0, a0)
    own3 = move(b3, MID_TO_MID)
    swap3 = move(b3, NEIGHBOUR)
    one.swap()
    two = batch((0, ca, own0), (0, a0, own0))
    two.send()
    two.keep()
    rows1 = rows_of(1)

    order.phase(own3, swap3, rows1, one.other)
    s3, s1 = one.finish()
    relay3 = move(swap3, MID_TO_MID)
    both3 = exchange(b0, own3)
    two.swap()
    b2 = columns_of(2)
    three = batch((3, ca, swap3), (0, ca, b0), (0, a0, b0))
    three.send()
    three.keep()
    rows2 = rows_of(2)

    order.phase(relay3, both3, rows2, b2, two.other)
    f0 = two.finish()
    relay0 = move(both3, MID_TO_MID)
    both4 = exchange(rows1.reshape(b0.shape), relay3)
    three.swap()
    four = batch((2, ca, b2), (0, ca, both3), (3, ca, jnp.where(at_end, order.open(both3), own3)))
    four.send()
    four.keep()

    order.phase(relay0, both4, three.other)
    n3, *s0 = three.finish()
    a1 = both4.reshape(a0.shape)
    own1 = move(b1, MID_TO_MID)
    both5 = exchange(rows2.reshape(b0.shape), jnp.concatenate([f0[1], s0[1]] * 2).reshape(b0.shape))
    four.swap()
    five = batch((0, ca, relay0), (0, a0, relay0), (3, ca, jnp.where(at_end, order.open(both4), relay3)))
    five.send()
    five.keep()

    order.phase(own1, both5, four.other)
    s2, n0, f3 = four.finish()
    a2 = both5.reshape(a0.shape)
    backs = both5.reshape(8, quarter, 2 * columns)
    f0_back, s0_back = backs[0:2], backs[2:4]
    own2 = move(b2, MID_TO_MID)
    swap1 = move(b1, NEIGHBOUR)
    x03a = cross((s0[0], home(f0[0], f0_back)), (s3, f3))
    five.swap()
    six = batch((1, ca, own1), (1, a1, own1))
    six.send()
    six.keep()

    order.phase(own2, swap1, x03a[1], five.other)
    *g0, g3 = five.finish()
    relay1 = move(swap1, MID_TO_MID)
    swap2 = move(b2, NEIGHBOUR)
    six.swap()
    seven = batch((2, ca, own2), (2, a2, own2), (1, ca, swap1))
    seven.send()
    seven.keep()

    order.phase(relay1, swap2, six.other)
    f1 = six.finish()
    relay2 = [move(swap2[:, :columns], MID_TO_MID)]
    backs = move(jnp.concatenate([g0[1], f1[1]]), MID_TO_END)
    seven.swap()
    eight = batch((1, ca, relay1), (1, a1, relay1), (2, ca, swap2))
    eight.send()
    eight.keep()

    order.phase(relay2[0], backs, seven.other)
    *f2, n1 = seven.finish()
    relay2.append(move(swap2[:, columns:], MID_TO_MID))
    gathered = lax.all_gather(order.open(ladder_amplitudes), "vir", axis=0, tiled=True)
    g0_back, f1_back = backs[0:2], backs[2:4]
    f2_back = move(f2[1], MID_TO_END)
    x01 = cross((home(n0, s0_back), home(g0[0], g0_back)), (s1, home(f1[0], f1_back)), (n3, g3))
    eight.swap()
    nine = batch((2, ca, relay2[0]), (2, a2, relay2[0]))
    nine.send()
    nine.keep()

    order.phase(relay2[1], f2_back, x01[1], eight.other)
    *g1, n2 = eight.finish()
    nine.swap()
    ten = batch((2, ca, relay2[1]), (2, a2, relay2[1]))
    ten.send()
    ten.keep()
    ten.swap()
    x2a = cross((s2, home(f2[0], f2_back)))
    near1_in, near2_in = over(n1), over(n2)
    x1b = straight(n1, near1_in, g1)
    x2b = [straight(n2, near2_in, nine.finish(), slice(0, columns))]
    out = None
    for j in range(2):
        out = put(0, j, [(x03a, 0, j), (x01, 1, j), (x2a, 0, j), (x03a, 1, j)], out)
    x2b.append(straight(n2, near2_in, ten.finish(), slice(columns, 2 * columns)))
    partial_ladder = order.step(jnp.dot(
        order.follow(gathered), ladder_integrals, preferred_element_type=F32,
    ).astype(BF16))
    ladder_residual = lax.psum_scatter(partial_ladder, ("occ", "ka"), scatter_dimension=0, tiled=True)
    for j in range(2):
        out = put(1, j, [(x01, 0, j), (x1b, 0, j), (x2b[j], 0, 0), (x01, 2, j)], out)
    return ladder_residual, out


def regroup(blocks):
    local_rows = blocks.shape[1]
    first_irrep = lax.axis_index("vir") * local_rows
    pieces = []
    for local_index in range(local_rows):
        permuted = jnp.bitwise_xor(first_irrep + local_index, jnp.arange(8, dtype=jnp.int32))
        pieces.append(jnp.take(blocks[:, local_index], permuted, axis=2))
    stacked = jnp.stack(pieces, axis=1)
    return jnp.transpose(stacked, (3, 1, 2, 0, 4))


def any_local(ladder_amplitudes, ladder_integrals, cycle_amplitudes, cycle_integrals):
    partial_ladder = jnp.dot(
        lax.all_gather(ladder_amplitudes, "vir", axis=0, tiled=True),
        ladder_integrals,
        preferred_element_type=F32,
    )
    summed_ladder = lax.psum_scatter(
        partial_ladder.astype(BF16), ("occ", "ka"), scatter_dimension=0, tiled=True
    )
    partial_cycle = jnp.einsum(
        "gaxk,gkny->gaxny",
        cycle_amplitudes,
        lax.all_gather(cycle_integrals, "vir", axis=2, tiled=True),
        preferred_element_type=F32,
    )
    summed_cycle = lax.psum_scatter(
        partial_cycle.astype(BF16), "ka", scatter_dimension=2, tiled=True
    )
    arranged = regroup(summed_cycle)
    cycle_residual = lax.all_to_all(arranged, "occ", split_axis=0, concat_axis=3, tiled=True)
    return (summed_ladder, cycle_residual)


def solution(mesh):
    line = (mesh.shape["vir"], mesh.shape["occ"], mesh.shape["ka"]) == (4, 2, 4)
    placed = (
        P("vir", ("occ", "ka")),
        P(("occ", "ka"), "vir"),
        P("occ", "vir", None, "ka"),
        P("occ", "ka", "vir", None),
    )
    return jax.shard_map(
        line_local if line else any_local,
        mesh=mesh,
        in_specs=placed,
        out_specs=(P(("occ", "ka"), "vir"), P("occ", "vir", "ka", None, None)),
        check_vma=False,
    )
```

```python
import jax
import jax.numpy as jnp
from jax import lax
from jax.experimental import pallas as pl
from jax.experimental.pallas import tpu as pltpu
from jax.sharding import PartitionSpec as P

F32, BF16 = jnp.float32, jnp.bfloat16

END_TO_MID = [(0, 1), (3, 2)]
MID_TO_MID = [(1, 2), (2, 1)]
MID_TO_END = [(1, 0), (2, 3)]
RELATIVE = (0, 2, 1, 3)
OTHER_CORE = [(0, 1), (1, 0), (2, 3), (3, 2)]
OTHER_Y = [(0, 2), (2, 0), (1, 3), (3, 1)]
OTHER_OCC = [(0, 1), (1, 0)]
NEIGHBOUR = [(0, 1), (1, 0), (2, 3), (3, 2)]
ROOM = 60 << 20
CHEAP = pl.CostEstimate(flops=1 << 20, bytes_accessed=1 << 16, transcendentals=0)


def after(value, *earlier):
    return lax.optimization_barrier((value, *earlier))[0]


def dot_rows(lhs, rhs):
    return jnp.dot(lhs.reshape(-1, lhs.shape[-1]), rhs, preferred_element_type=F32)


def operands(products, first):
    specs, arrays, places = [], [], {}
    for place, (irrep, lhs, _) in enumerate(products):
        rows, depth = lhs.shape[-2] // 4, lhs.shape[-1]

        def quarter(p, r, where, place=place):
            return where[first + jnp.where(p == place, r, jnp.where(p < place, 0, 1))]
        if lhs.ndim == 4:
            specs.append(pl.BlockSpec(
                (1, 2, rows, depth), lambda p, r, where, g=irrep, q=quarter: (g, 0, q(p, r, where), 0)))
        else:
            specs.append(pl.BlockSpec((2, rows, depth), lambda p, r, where, q=quarter: (0, q(p, r, where), 0)))
        arrays.append(lhs)
    for _, _, rhs in products:
        if id(rhs) not in places:
            places[id(rhs)] = len(arrays)
            specs.append(pl.BlockSpec(rhs.shape, lambda p, r, where: (0, 0)))
            arrays.append(rhs)
    return specs, arrays, [places[id(rhs)] for _, _, rhs in products]


def run_products(refs, columns_at, use):
    for place, at in enumerate(columns_at):
        @pl.when(pl.program_id(0) == place)
        def _():
            use(dot_rows(refs[place][...], refs[at][...]))


def send_products(where, products):
    specs, arrays, columns_at = operands(products, 2)
    count, rows, columns = len(products), products[0][1].shape[-2] // 2, products[0][2].shape[1]

    def kernel(where_ref, *refs):
        def use(value):
            for quarter, out in enumerate(refs[-2:]):
                @pl.when(pl.program_id(1) == quarter)
                def _():
                    out[0] = value.astype(BF16)
        run_products(refs, columns_at, use)

    return pl.pallas_call(
        kernel,
        out_shape=(jax.ShapeDtypeStruct((count, rows, columns), BF16),) * 2,
        grid_spec=pltpu.PrefetchScalarGridSpec(
            num_scalar_prefetch=1,
            grid=(count, 2),
            in_specs=specs,
            out_specs=(pl.BlockSpec((1, rows, columns), lambda p, r, where: (p, 0, 0)),) * 2,
        ),
        compiler_params=pltpu.CompilerParams(vmem_limit_bytes=ROOM),
        cost_estimate=CHEAP,
        name="send_products",
    )(where, *arrays)


def keep_products(where, products, arrived):
    specs, arrays, columns_at = operands(products, 0)
    count, rows, columns = len(products), products[0][1].shape[-2] // 2, products[0][2].shape[1]

    def kernel(where_ref, *refs):
        def use(value):
            for quarter, (arrived_ref, out) in enumerate(zip(refs[-4:-2], refs[-2:])):
                @pl.when(pl.program_id(1) == quarter)
                def _():
                    out[0] = (value + arrived_ref[0].astype(F32)).astype(BF16)
        run_products(refs, columns_at, use)

    return pl.pallas_call(
        kernel,
        out_shape=(jax.ShapeDtypeStruct((count, rows, columns), BF16),) * 2,
        grid_spec=pltpu.PrefetchScalarGridSpec(
            num_scalar_prefetch=1,
            grid=(count, 2),
            in_specs=specs + [pl.BlockSpec((1, rows, columns), lambda p, r, where: (p, 0, 0))] * 2,
            out_specs=(pl.BlockSpec((1, rows, columns), lambda p, r, where: (p, 0, 0)),) * 2,
        ),
        compiler_params=pltpu.CompilerParams(vmem_limit_bytes=ROOM),
        cost_estimate=CHEAP,
        name="keep_products",
    )(where, *arrays, *arrived)


def place(base, parity, kept, arrived, out, shape):
    count = len(kept)
    rows, columns = shape[2], shape[4]
    block = rows // 2

    def kernel(base_ref, *refs):
        out_ref, wide = refs[-2:]
        first = base_ref[1] == 0
        for index in range(count):
            mine, theirs = refs[index][0].astype(F32), refs[count + index][0].astype(F32)
            wide[:, index, :] = jnp.where(first, mine, theirs)
            wide[:, count + index, :] = jnp.where(first, theirs, mine)
        out_ref[0, 0] = wide[...].astype(BF16)

    pieces = kept + arrived
    specs = [
        pl.BlockSpec((1, block, columns), lambda a, i, base, j=j, first=first: (first + a, i, j))
        for _, first, j in pieces]
    extra = [] if out is None else [out]
    return pl.pallas_call(
        kernel,
        out_shape=jax.ShapeDtypeStruct(shape, BF16),
        grid_spec=pltpu.PrefetchScalarGridSpec(
            num_scalar_prefetch=1,
            grid=(2, rows // block),
            in_specs=specs + [pl.BlockSpec(memory_space=pl.ANY)] * len(extra),
            out_specs=pl.BlockSpec(
                (1, 1, block, 2 * count, columns),
                lambda a, i, base: (base[0] + (a + parity) % 2, a, i, 0, 0)),
            scratch_shapes=[pltpu.VMEM((block, 2 * count, columns), F32)],
        ),
        input_output_aliases={1 + 2 * count: 0} if extra else {},
        compiler_params=pltpu.CompilerParams(vmem_limit_bytes=ROOM),
        cost_estimate=CHEAP,
        name="place",
    )(base, *[array for array, _, _ in pieces], *extra)


class Order:
    def __init__(self):
        self.before, self.edge = [], []

    def follow(self, value):
        return after(value, *self.before) if self.before else value

    def step(self, value):
        self.before = [value]
        return value

    def phase(self, *values):
        self.before = self.before + list(values)
        self.edge = self.before

    def open(self, value):
        return after(value, *self.edge) if self.edge else value


class Batch:
    def __init__(self, order, where, *products):
        self.order, self.where, self.products = order, where, products

    def send(self):
        followed = {id(rhs): rhs for _, _, rhs in self.products}
        followed = {key: self.order.follow(rhs) for key, rhs in followed.items()}
        self.products = [(irrep, lhs, followed[id(rhs)]) for irrep, lhs, rhs in self.products]
        parts = send_products(self.where, self.products)
        self.order.step(parts[1])
        self.arrived = [lax.ppermute(part, "ka", OTHER_CORE) for part in parts]

    def keep(self):
        arrived = [self.order.follow(part) for part in self.arrived]
        self.own, self.away = keep_products(self.where, self.products, arrived)
        self.order.step(self.away)

    def swap(self):
        self.other = lax.ppermute(self.order.open(self.away), "ka", OTHER_Y)

    def finish(self):
        total = (self.own.astype(F32) + self.order.open(self.other).astype(F32)).astype(BF16)
        count, rows, columns = total.shape
        return [total[p].reshape(2, rows // 2, columns) for p in range(count)]


def line_local(ladder_amplitudes, ladder_integrals, cycle_amplitudes, cycle_integrals):
    vir, occ, ka = (lax.axis_index(name) for name in ("vir", "occ", "ka"))
    irreps, rows_here, group, depth = cycle_amplitudes.shape
    quarter = group // 4
    columns = cycle_integrals.shape[3]
    at_end = (vir == 0) | (vir == 3)
    where = jnp.bitwise_xor(ka, jnp.array(RELATIVE, jnp.int32))
    order = Order()

    def columns_of(g):
        return order.open(cycle_integrals)[g].reshape(depth, 2 * columns)

    def exchange(inwards, outwards):
        return move(jnp.where(at_end, order.open(inwards), order.open(outwards)), NEIGHBOUR)

    def batch(*products):
        return Batch(order, where, *products)

    def move(value, route):
        return lax.ppermute(order.open(value), "vir", route)

    def cross(*pairs):
        pairs = [(order.open(near), order.open(far)) for near, far in pairs]
        away = jnp.concatenate([jnp.where(occ == 0, far, near) for near, far in pairs])
        return [jnp.where(occ == 0, near, far) for near, far in pairs], lax.ppermute(away, "occ", OTHER_OCC)

    def home(mine, back):
        return jnp.where(at_end, order.open(back), order.open(mine))

    low = jnp.where((occ == 0) | at_end, 0, 2).astype(jnp.int32)
    shape = (8 // 2, rows_here, quarter, 2 * irreps, columns)

    def put(half, j, crossed, out):
        base = jnp.stack([low if half == 0 else 2 - low, occ.astype(jnp.int32)])
        kept = [(pair[0][index], 0, jj) for pair, index, jj in crossed]
        arrived = [(pair[1], 2 * index, jj) for pair, index, jj in crossed]
        return order.step(place(base, j, kept, arrived, out, shape))

    def rows_of(g):
        return order.open(cycle_amplitudes)[g]

    def straight(near, near_in, rows, one=slice(None)):
        own_rows, foreign = (order.open(value) for value in rows)
        first = lax.ppermute(jnp.where(occ == 0, own_rows, foreign), ("vir", "occ"), [(2, 3), (4, 5), (3, 1), (5, 7)])
        second = lax.ppermute(foreign, ("vir", "occ"), [(2, 1), (4, 7)])
        kept = jnp.where(occ == 0, near[..., one], jnp.where(at_end, first, own_rows))
        arrived = jnp.where(occ == 0, near_in[..., one], jnp.where(at_end, second, first))
        return [kept], arrived

    def over(near):
        return lax.ppermute(order.open(near), "occ", [(1, 0)])

    ca = cycle_amplitudes
    gathered = lax.all_gather(ladder_amplitudes, "vir", axis=0, tiled=True)
    b0 = columns_of(0)
    order.phase(b0)
    own0 = move(b0, MID_TO_MID)
    a0 = move(rows_of(0), END_TO_MID)
    b3, b1, b2 = columns_of(3), columns_of(1), columns_of(2)
    one = batch((3, ca, b3), (1, ca, b1), (2, ca, b2))
    one.send()
    one.keep()

    order.phase(own0, a0, gathered)
    own3 = move(b3, MID_TO_MID)
    swap3 = move(b3, NEIGHBOUR)
    one.swap()
    two = batch((0, ca, own0), (0, a0, own0))
    partial_ladder = order.step(jnp.dot(
        order.follow(gathered), ladder_integrals, preferred_element_type=F32,
    ).astype(BF16))
    ladder_residual = lax.psum_scatter(partial_ladder, ("occ", "ka"), scatter_dimension=0, tiled=True)
    two.send()
    two.keep()
    rows1 = rows_of(1)

    order.phase(own3, swap3, rows1, one.other)
    s3, s1, s2 = one.finish()
    relay3 = move(swap3, MID_TO_MID)
    both3 = exchange(b0, own3)
    two.swap()
    three = batch((3, ca, swap3), (0, ca, b0), (0, a0, b0))
    three.send()
    three.keep()
    rows2 = rows_of(2)

    order.phase(relay3, both3, rows2, two.other)
    f0 = two.finish()
    relay0 = move(both3, MID_TO_MID)
    both4 = exchange(rows1.reshape(b0.shape), relay3)
    three.swap()
    four = batch((0, ca, both3), (3, ca, jnp.where(at_end, order.open(both3), own3)))
    four.send()
    four.keep()

    order.phase(relay0, both4, three.other)
    n3, *s0 = three.finish()
    a1 = both4.reshape(a0.shape)
    own1 = move(b1, MID_TO_MID)
    both5 = exchange(rows2.reshape(b0.shape), jnp.concatenate([f0[1], s0[1]] * 2).reshape(b0.shape))
    four.swap()
    five = batch((0, ca, relay0), (0, a0, relay0), (3, ca, jnp.where(at_end, order.open(both4), relay3)))
    five.send()
    five.keep()

    order.phase(own1, both5, four.other, ladder_residual)
    n0, f3 = four.finish()
    a2 = both5.reshape(a0.shape)
    backs = both5.reshape(8, quarter, 2 * columns)
    f0_back, s0_back = backs[0:2], backs[2:4]
    own2 = move(b2, MID_TO_MID)
    swap1 = move(b1, NEIGHBOUR)
    five.swap()
    six = batch((1, ca, own1), (1, a1, own1))
    six.send()
    six.keep()

    order.phase(own2, swap1, five.other)
    *g0, g3 = five.finish()
    relay1 = move(swap1, MID_TO_MID)
    swap2 = move(b2, NEIGHBOUR)
    six.swap()
    seven = batch((2, ca, own2), (2, a2, own2), (1, ca, swap1))
    seven.send()
    seven.keep()

    order.phase(relay1, swap2, six.other)
    f1 = six.finish()
    relay2 = [move(swap2[:, :columns], MID_TO_MID)]
    backs = move(jnp.concatenate([g0[1], f1[1]]), MID_TO_END)
    x03a = cross((s0[0], home(f0[0], f0_back)), (s3, f3))
    seven.swap()
    eight = batch((1, ca, relay1), (1, a1, relay1), (2, ca, swap2))
    eight.send()
    eight.keep()

    order.phase(relay2[0], backs, x03a[1], seven.other)
    *f2, n1 = seven.finish()
    relay2.append(move(swap2[:, columns:], MID_TO_MID))
    g0_back, f1_back = backs[0:2], backs[2:4]
    f2_back = move(f2[1], MID_TO_END)
    x01 = cross((home(n0, s0_back), home(g0[0], g0_back)), (s1, home(f1[0], f1_back)), (n3, g3))
    eight.swap()
    nine = batch((2, ca, relay2[0]), (2, a2, relay2[0]))
    nine.send()
    nine.keep()

    order.phase(relay2[1], f2_back, x01[1], eight.other)
    *g1, n2 = eight.finish()
    nine.swap()
    ten = batch((2, ca, relay2[1]), (2, a2, relay2[1]))
    ten.send()
    ten.keep()
    ten.swap()
    x2a = cross((s2, home(f2[0], f2_back)))
    near_in = over(jnp.concatenate([n1, n2]))
    near1_in, near2_in = near_in[0:2], near_in[2:4]
    x1b = straight(n1, near1_in, g1)
    x2b = [straight(n2, near2_in, nine.finish(), slice(0, columns))]
    out = None
    for j in range(2):
        out = put(0, j, [(x03a, 0, j), (x01, 1, j), (x2a, 0, j), (x03a, 1, j)], out)
    x2b.append(straight(n2, near2_in, ten.finish(), slice(columns, 2 * columns)))
    for j in range(2):
        out = put(1, j, [(x01, 0, j), (x1b, 0, j), (x2b[j], 0, 0), (x01, 2, j)], out)
    return ladder_residual, out


def regroup(blocks):
    local_rows = blocks.shape[1]
    first_irrep = lax.axis_index("vir") * local_rows
    pieces = []
    for local_index in range(local_rows):
        permuted = jnp.bitwise_xor(first_irrep + local_index, jnp.arange(8, dtype=jnp.int32))
        pieces.append(jnp.take(blocks[:, local_index], permuted, axis=2))
    stacked = jnp.stack(pieces, axis=1)
    return jnp.transpose(stacked, (3, 1, 2, 0, 4))


def any_local(ladder_amplitudes, ladder_integrals, cycle_amplitudes, cycle_integrals):
    partial_ladder = jnp.dot(
        lax.all_gather(ladder_amplitudes, "vir", axis=0, tiled=True),
        ladder_integrals,
        preferred_element_type=F32,
    )
    summed_ladder = lax.psum_scatter(
        partial_ladder.astype(BF16), ("occ", "ka"), scatter_dimension=0, tiled=True
    )
    partial_cycle = jnp.einsum(
        "gaxk,gkny->gaxny",
        cycle_amplitudes,
        lax.all_gather(cycle_integrals, "vir", axis=2, tiled=True),
        preferred_element_type=F32,
    )
    summed_cycle = lax.psum_scatter(
        partial_cycle.astype(BF16), "ka", scatter_dimension=2, tiled=True
    )
    arranged = regroup(summed_cycle)
    cycle_residual = lax.all_to_all(arranged, "occ", split_axis=0, concat_axis=3, tiled=True)
    return (summed_ladder, cycle_residual)


def solution(mesh):
    line = (mesh.shape["vir"], mesh.shape["occ"], mesh.shape["ka"]) == (4, 2, 4)
    placed = (
        P("vir", ("occ", "ka")),
        P(("occ", "ka"), "vir"),
        P("occ", "vir", None, "ka"),
        P("occ", "ka", "vir", None),
    )
    return jax.shard_map(
        line_local if line else any_local,
        mesh=mesh,
        in_specs=placed,
        out_specs=(P(("occ", "ka"), "vir"), P("occ", "vir", "ka", None, None)),
        check_vma=False,
    )
```

```python
import jax
import jax.numpy as jnp
from jax import lax
from jax.experimental import pallas as pl
from jax.experimental.pallas import tpu as pltpu
from jax.sharding import PartitionSpec as P

F32, BF16 = jnp.float32, jnp.bfloat16

END_TO_MID = [(0, 1), (3, 2)]
MID_TO_MID = [(1, 2), (2, 1)]
MID_TO_END = [(1, 0), (2, 3)]
RELATIVE = (0, 2, 1, 3)
OTHER_CORE = [(0, 1), (1, 0), (2, 3), (3, 2)]
OTHER_Y = [(0, 2), (2, 0), (1, 3), (3, 1)]
OTHER_OCC = [(0, 1), (1, 0)]
NEIGHBOUR = [(0, 1), (1, 0), (2, 3), (3, 2)]
ROOM = 60 << 20
CHEAP = pl.CostEstimate(flops=1 << 20, bytes_accessed=1 << 16, transcendentals=0)


def after(value, *earlier):
    return lax.optimization_barrier((value, *earlier))[0]


def dot_rows(lhs, rhs):
    return jnp.dot(lhs.reshape(-1, lhs.shape[-1]), rhs, preferred_element_type=F32)


def operands(products, first):
    specs, arrays, places = [], [], {}
    for place, (irrep, lhs, _) in enumerate(products):
        rows, depth = lhs.shape[-2] // 4, lhs.shape[-1]

        def quarter(p, r, where, place=place):
            return where[first + jnp.where(p == place, r, jnp.where(p < place, 0, 1))]
        if lhs.ndim == 4:
            specs.append(pl.BlockSpec(
                (1, 2, rows, depth), lambda p, r, where, g=irrep, q=quarter: (g, 0, q(p, r, where), 0)))
        else:
            specs.append(pl.BlockSpec((2, rows, depth), lambda p, r, where, q=quarter: (0, q(p, r, where), 0)))
        arrays.append(lhs)
    for _, _, rhs in products:
        if id(rhs) not in places:
            places[id(rhs)] = len(arrays)
            specs.append(pl.BlockSpec(rhs.shape, lambda p, r, where: (0, 0)))
            arrays.append(rhs)
    return specs, arrays, [places[id(rhs)] for _, _, rhs in products]


def run_products(refs, columns_at, use):
    for place, at in enumerate(columns_at):
        @pl.when(pl.program_id(0) == place)
        def _():
            use(dot_rows(refs[place][...], refs[at][...]))


def send_products(where, products):
    specs, arrays, columns_at = operands(products, 2)
    count, rows, columns = len(products), products[0][1].shape[-2] // 2, products[0][2].shape[1]

    def kernel(where_ref, *refs):
        def use(value):
            for quarter, out in enumerate(refs[-2:]):
                @pl.when(pl.program_id(1) == quarter)
                def _():
                    out[0] = value.astype(BF16)
        run_products(refs, columns_at, use)

    return pl.pallas_call(
        kernel,
        out_shape=(jax.ShapeDtypeStruct((count, rows, columns), BF16),) * 2,
        grid_spec=pltpu.PrefetchScalarGridSpec(
            num_scalar_prefetch=1,
            grid=(count, 2),
            in_specs=specs,
            out_specs=(pl.BlockSpec((1, rows, columns), lambda p, r, where: (p, 0, 0)),) * 2,
        ),
        compiler_params=pltpu.CompilerParams(vmem_limit_bytes=ROOM),
        cost_estimate=CHEAP,
        name="send_products",
    )(where, *arrays)


def keep_products(where, products, arrived):
    specs, arrays, columns_at = operands(products, 0)
    count, rows, columns = len(products), products[0][1].shape[-2] // 2, products[0][2].shape[1]

    def kernel(where_ref, *refs):
        def use(value):
            for quarter, (arrived_ref, out) in enumerate(zip(refs[-4:-2], refs[-2:])):
                @pl.when(pl.program_id(1) == quarter)
                def _():
                    out[0] = (value + arrived_ref[0].astype(F32)).astype(BF16)
        run_products(refs, columns_at, use)

    return pl.pallas_call(
        kernel,
        out_shape=(jax.ShapeDtypeStruct((count, rows, columns), BF16),) * 2,
        grid_spec=pltpu.PrefetchScalarGridSpec(
            num_scalar_prefetch=1,
            grid=(count, 2),
            in_specs=specs + [pl.BlockSpec((1, rows, columns), lambda p, r, where: (p, 0, 0))] * 2,
            out_specs=(pl.BlockSpec((1, rows, columns), lambda p, r, where: (p, 0, 0)),) * 2,
        ),
        compiler_params=pltpu.CompilerParams(vmem_limit_bytes=ROOM),
        cost_estimate=CHEAP,
        name="keep_products",
    )(where, *arrays, *arrived)


def place(base, parity, kept, arrived, out, shape):
    count = len(kept)
    rows, columns = shape[2], shape[4]
    block = rows // 2

    def kernel(base_ref, *refs):
        out_ref, wide = refs[-2:]
        first = base_ref[1] == 0
        for index in range(count):
            mine, theirs = refs[index][0].astype(F32), refs[count + index][0].astype(F32)
            wide[:, index, :] = jnp.where(first, mine, theirs)
            wide[:, count + index, :] = jnp.where(first, theirs, mine)
        out_ref[0, 0] = wide[...].astype(BF16)

    pieces = kept + arrived
    specs = [
        pl.BlockSpec((1, block, columns), lambda a, i, base, j=j, first=first: (first + a, i, j))
        for _, first, j in pieces]
    extra = [] if out is None else [out]
    return pl.pallas_call(
        kernel,
        out_shape=jax.ShapeDtypeStruct(shape, BF16),
        grid_spec=pltpu.PrefetchScalarGridSpec(
            num_scalar_prefetch=1,
            grid=(2, rows // block),
            in_specs=specs + [pl.BlockSpec(memory_space=pl.ANY)] * len(extra),
            out_specs=pl.BlockSpec(
                (1, 1, block, 2 * count, columns),
                lambda a, i, base: (base[0] + (a + parity) % 2, a, i, 0, 0)),
            scratch_shapes=[pltpu.VMEM((block, 2 * count, columns), F32)],
        ),
        input_output_aliases={1 + 2 * count: 0} if extra else {},
        compiler_params=pltpu.CompilerParams(vmem_limit_bytes=ROOM),
        cost_estimate=CHEAP,
        name="place",
    )(base, *[array for array, _, _ in pieces], *extra)


class Order:
    def __init__(self):
        self.before, self.edge = [], []

    def follow(self, value):
        return after(value, *self.before) if self.before else value

    def step(self, value):
        self.before = [value]
        return value

    def phase(self, *values):
        self.before = self.before + list(values)
        self.edge = self.before

    def open(self, value):
        return after(value, *self.edge) if self.edge else value


class Batch:
    def __init__(self, order, where, *products):
        self.order, self.where, self.products = order, where, products

    def send(self):
        followed = {id(rhs): rhs for _, _, rhs in self.products}
        followed = {key: self.order.follow(rhs) for key, rhs in followed.items()}
        self.products = [(irrep, lhs, followed[id(rhs)]) for irrep, lhs, rhs in self.products]
        parts = send_products(self.where, self.products)
        self.order.step(parts[1])
        self.arrived = [lax.ppermute(part, "ka", OTHER_CORE) for part in parts]

    def keep(self):
        arrived = [self.order.follow(part) for part in self.arrived]
        self.own, self.away = keep_products(self.where, self.products, arrived)
        self.order.step(self.away)

    def swap(self):
        self.other = lax.ppermute(self.order.open(self.away), "ka", OTHER_Y)

    def finish(self):
        total = (self.own.astype(F32) + self.order.open(self.other).astype(F32)).astype(BF16)
        count, rows, columns = total.shape
        return [total[p].reshape(2, rows // 2, columns) for p in range(count)]


def line_local(ladder_amplitudes, ladder_integrals, cycle_amplitudes, cycle_integrals):
    vir, occ, ka = (lax.axis_index(name) for name in ("vir", "occ", "ka"))
    irreps, rows_here, group, depth = cycle_amplitudes.shape
    quarter = group // 4
    columns = cycle_integrals.shape[3]
    at_end = (vir == 0) | (vir == 3)
    where = jnp.bitwise_xor(ka, jnp.array(RELATIVE, jnp.int32))
    order = Order()

    def columns_of(g):
        return order.open(cycle_integrals)[g].reshape(depth, 2 * columns)

    def exchange(inwards, outwards):
        return move(jnp.where(at_end, order.open(inwards), order.open(outwards)), NEIGHBOUR)

    def batch(*products):
        return Batch(order, where, *products)

    def move(value, route):
        return lax.ppermute(order.open(value), "vir", route)

    def cross(*pairs):
        pairs = [(order.open(near), order.open(far)) for near, far in pairs]
        away = jnp.concatenate([jnp.where(occ == 0, far, near) for near, far in pairs])
        return [jnp.where(occ == 0, near, far) for near, far in pairs], lax.ppermute(away, "occ", OTHER_OCC)

    def home(mine, back):
        return jnp.where(at_end, order.open(back), order.open(mine))

    low = jnp.where((occ == 0) | at_end, 0, 2).astype(jnp.int32)
    shape = (8 // 2, rows_here, quarter, 2 * irreps, columns)

    def put(half, j, crossed, out):
        base = jnp.stack([low if half == 0 else 2 - low, occ.astype(jnp.int32)])
        kept = [(pair[0][index], 0, jj) for pair, index, jj in crossed]
        arrived = [(pair[1], 2 * index, jj) for pair, index, jj in crossed]
        return order.step(place(base, j, kept, arrived, out, shape))

    def rows_of(g):
        return order.open(cycle_amplitudes)[g]

    def straight(near, near_in, rows, one=slice(None)):
        own_rows, foreign = (order.open(value) for value in rows)
        first = lax.ppermute(jnp.where(occ == 0, own_rows, foreign), ("vir", "occ"), [(2, 3), (4, 5), (3, 1), (5, 7)])
        second = lax.ppermute(foreign, ("vir", "occ"), [(2, 1), (4, 7)])
        kept = jnp.where(occ == 0, near[..., one], jnp.where(at_end, first, own_rows))
        arrived = jnp.where(occ == 0, near_in[..., one], jnp.where(at_end, second, first))
        return [kept], arrived

    def over(near):
        return lax.ppermute(order.open(near), "occ", [(1, 0)])

    ca = cycle_amplitudes
    ladder_near = move(ladder_amplitudes, NEIGHBOUR)
    ladder_far = move(ladder_amplitudes, MID_TO_MID)
    b0 = columns_of(0)

    order.phase(ladder_near, ladder_far, b0)
    ladder_last = move(ladder_near, MID_TO_MID)
    on_far = move(ladder_far, MID_TO_END)
    b3, b1, b2 = columns_of(3), columns_of(1), columns_of(2)

    order.phase(ladder_last, on_far, b3, b1, b2)
    on_last = move(ladder_last, MID_TO_END)
    own0 = move(b0, MID_TO_MID)
    a0 = move(rows_of(0), END_TO_MID)
    one = batch((3, ca, b3), (1, ca, b1), (2, ca, b2))
    one.send()
    one.keep()

    order.phase(own0, a0, on_last)
    own3 = move(b3, MID_TO_MID)
    swap3 = move(b3, NEIGHBOUR)
    one.swap()
    two = batch((0, ca, own0), (0, a0, own0))
    rows = jnp.concatenate([
        ladder_amplitudes, ladder_near,
        jnp.where(at_end, order.open(on_far), ladder_far), jnp.where(at_end, order.open(on_last), ladder_last)])
    partial_ladder = order.step(jnp.dot(
        order.follow(rows), ladder_integrals, preferred_element_type=F32).astype(BF16))
    plane = jnp.arange(4)
    held = jnp.where(
        plane // 2 == vir // 2, jnp.where(plane == vir, 0, 1), jnp.where((plane == 1) | (plane == 2), 2, 3))
    step = ladder_amplitudes.shape[0]
    partial_ladder = jnp.concatenate([
        lax.dynamic_slice_in_dim(partial_ladder, held[w] * step, step, 0) for w in range(4)])
    ladder_residual = lax.psum_scatter(partial_ladder, ("occ", "ka"), scatter_dimension=0, tiled=True)
    two.send()
    two.keep()
    rows1 = rows_of(1)

    order.phase(own3, swap3, rows1, one.other)
    s3, s1, s2 = one.finish()
    relay3 = move(swap3, MID_TO_MID)
    both3 = exchange(b0, own3)
    two.swap()
    three = batch((3, ca, swap3), (0, ca, b0), (0, a0, b0))
    three.send()
    three.keep()
    rows2 = rows_of(2)

    order.phase(relay3, both3, rows2, two.other)
    f0 = two.finish()
    relay0 = move(both3, MID_TO_MID)
    both4 = exchange(rows1.reshape(b0.shape), relay3)
    three.swap()
    four = batch((0, ca, both3), (3, ca, jnp.where(at_end, order.open(both3), own3)))
    four.send()
    four.keep()

    order.phase(relay0, both4, three.other, f0[1])
    n3, *s0 = three.finish()
    a1 = both4.reshape(a0.shape)
    own1 = move(b1, MID_TO_MID)
    both5 = exchange(rows2.reshape(b0.shape), jnp.concatenate([f0[1], s0[1]] * 2).reshape(b0.shape))
    four.swap()
    five = batch((0, ca, relay0), (0, a0, relay0), (3, ca, jnp.where(at_end, order.open(both4), relay3)))
    five.send()
    five.keep()

    order.phase(own1, both5, four.other, ladder_residual)
    n0, f3 = four.finish()
    a2 = both5.reshape(a0.shape)
    backs = both5.reshape(8, quarter, 2 * columns)
    f0_back, s0_back = backs[0:2], backs[2:4]
    own2 = move(b2, MID_TO_MID)
    swap1 = move(b1, NEIGHBOUR)
    five.swap()
    six = batch((1, ca, own1), (1, a1, own1))
    six.send()
    six.keep()

    order.phase(own2, swap1, five.other)
    *g0, g3 = five.finish()
    relay1 = move(swap1, MID_TO_MID)
    swap2 = move(b2, NEIGHBOUR)
    six.swap()
    seven = batch((2, ca, own2), (2, a2, own2), (1, ca, swap1))
    seven.send()
    seven.keep()

    order.phase(relay1, swap2, six.other)
    f1 = six.finish()
    relay2 = [move(swap2[:, :columns], MID_TO_MID)]
    backs = move(jnp.concatenate([g0[1], f1[1]]), MID_TO_END)
    x03a = cross((s0[0], home(f0[0], f0_back)), (s3, f3))
    seven.swap()
    eight = batch((1, ca, relay1), (1, a1, relay1), (2, ca, swap2))
    eight.send()
    eight.keep()

    order.phase(relay2[0], backs, x03a[1], seven.other)
    *f2, n1 = seven.finish()
    relay2.append(move(swap2[:, columns:], MID_TO_MID))
    g0_back, f1_back = backs[0:2], backs[2:4]
    f2_back = move(f2[1], MID_TO_END)
    x01 = cross((home(n0, s0_back), home(g0[0], g0_back)), (s1, home(f1[0], f1_back)), (n3, g3))
    eight.swap()
    nine = batch((2, ca, relay2[0]), (2, a2, relay2[0]))
    nine.send()
    nine.keep()

    order.phase(relay2[1], f2_back, x01[1], eight.other)
    *g1, n2 = eight.finish()
    nine.swap()
    ten = batch((2, ca, relay2[1]), (2, a2, relay2[1]))
    ten.send()
    ten.keep()
    ten.swap()
    x2a = cross((s2, home(f2[0], f2_back)))
    near_in = over(jnp.concatenate([n1, n2]))
    near1_in, near2_in = near_in[0:2], near_in[2:4]
    x1b = straight(n1, near1_in, g1)
    x2b = [straight(n2, near2_in, nine.finish(), slice(0, columns))]
    out = None
    for j in range(2):
        out = put(0, j, [(x03a, 0, j), (x01, 1, j), (x2a, 0, j), (x03a, 1, j)], out)
    x2b.append(straight(n2, near2_in, ten.finish(), slice(columns, 2 * columns)))
    for j in range(2):
        out = put(1, j, [(x01, 0, j), (x1b, 0, j), (x2b[j], 0, 0), (x01, 2, j)], out)
    return ladder_residual, out


def regroup(blocks):
    local_rows = blocks.shape[1]
    first_irrep = lax.axis_index("vir") * local_rows
    pieces = []
    for local_index in range(local_rows):
        permuted = jnp.bitwise_xor(first_irrep + local_index, jnp.arange(8, dtype=jnp.int32))
        pieces.append(jnp.take(blocks[:, local_index], permuted, axis=2))
    stacked = jnp.stack(pieces, axis=1)
    return jnp.transpose(stacked, (3, 1, 2, 0, 4))


def any_local(ladder_amplitudes, ladder_integrals, cycle_amplitudes, cycle_integrals):
    partial_ladder = jnp.dot(
        lax.all_gather(ladder_amplitudes, "vir", axis=0, tiled=True),
        ladder_integrals,
        preferred_element_type=F32,
    )
    summed_ladder = lax.psum_scatter(
        partial_ladder.astype(BF16), ("occ", "ka"), scatter_dimension=0, tiled=True
    )
    partial_cycle = jnp.einsum(
        "gaxk,gkny->gaxny",
        cycle_amplitudes,
        lax.all_gather(cycle_integrals, "vir", axis=2, tiled=True),
        preferred_element_type=F32,
    )
    summed_cycle = lax.psum_scatter(
        partial_cycle.astype(BF16), "ka", scatter_dimension=2, tiled=True
    )
    arranged = regroup(summed_cycle)
    cycle_residual = lax.all_to_all(arranged, "occ", split_axis=0, concat_axis=3, tiled=True)
    return (summed_ladder, cycle_residual)


def solution(mesh):
    line = (mesh.shape["vir"], mesh.shape["occ"], mesh.shape["ka"]) == (4, 2, 4)
    placed = (
        P("vir", ("occ", "ka")),
        P(("occ", "ka"), "vir"),
        P("occ", "vir", None, "ka"),
        P("occ", "ka", "vir", None),
    )
    return jax.shard_map(
        line_local if line else any_local,
        mesh=mesh,
        in_specs=placed,
        out_specs=(P(("occ", "ka"), "vir"), P("occ", "vir", "ka", None, None)),
        check_vma=False,
    )
```

```python
import jax
import jax.numpy as jnp
from jax import lax
from jax.experimental import pallas as pl
from jax.experimental.pallas import tpu as pltpu
from jax.sharding import PartitionSpec as P

F32, BF16 = jnp.float32, jnp.bfloat16

END_TO_MID = [(0, 1), (3, 2)]
MID_TO_MID = [(1, 2), (2, 1)]
MID_TO_END = [(1, 0), (2, 3)]
RELATIVE = (0, 2, 1, 3)
OTHER_CORE = [(0, 1), (1, 0), (2, 3), (3, 2)]
OTHER_Y = [(0, 2), (2, 0), (1, 3), (3, 1)]
OTHER_OCC = [(0, 1), (1, 0)]
NEIGHBOUR = [(0, 1), (1, 0), (2, 3), (3, 2)]
ROOM = 60 << 20
CHEAP = pl.CostEstimate(flops=1 << 20, bytes_accessed=1 << 16, transcendentals=0)


def after(value, *earlier):
    return lax.optimization_barrier((value, *earlier))[0]


def dot_rows(lhs, rhs):
    return jnp.dot(lhs.reshape(-1, lhs.shape[-1]), rhs, preferred_element_type=F32)


def operands(products, first):
    specs, arrays, places = [], [], {}
    for place, (irrep, lhs, _) in enumerate(products):
        rows, depth = lhs.shape[-2] // 4, lhs.shape[-1]

        def quarter(p, r, where, place=place):
            return where[first + jnp.where(p == place, r, jnp.where(p < place, 0, 1))]
        if lhs.ndim == 4:
            specs.append(pl.BlockSpec(
                (1, 2, rows, depth), lambda p, r, where, g=irrep, q=quarter: (g, 0, q(p, r, where), 0)))
        else:
            specs.append(pl.BlockSpec((2, rows, depth), lambda p, r, where, q=quarter: (0, q(p, r, where), 0)))
        arrays.append(lhs)
    for _, _, rhs in products:
        if id(rhs) not in places:
            places[id(rhs)] = len(arrays)
            specs.append(pl.BlockSpec(rhs.shape, lambda p, r, where: (0, 0)))
            arrays.append(rhs)
    return specs, arrays, [places[id(rhs)] for _, _, rhs in products]


def run_products(refs, columns_at, use):
    for place, at in enumerate(columns_at):
        @pl.when(pl.program_id(0) == place)
        def _():
            use(dot_rows(refs[place][...], refs[at][...]))


def send_products(where, products):
    specs, arrays, columns_at = operands(products, 2)
    count, rows, columns = len(products), products[0][1].shape[-2] // 2, products[0][2].shape[1]

    def kernel(where_ref, *refs):
        def use(value):
            for quarter, out in enumerate(refs[-2:]):
                @pl.when(pl.program_id(1) == quarter)
                def _():
                    out[0] = value.astype(BF16)
        run_products(refs, columns_at, use)

    return pl.pallas_call(
        kernel,
        out_shape=(jax.ShapeDtypeStruct((count, rows, columns), BF16),) * 2,
        grid_spec=pltpu.PrefetchScalarGridSpec(
            num_scalar_prefetch=1,
            grid=(count, 2),
            in_specs=specs,
            out_specs=(pl.BlockSpec((1, rows, columns), lambda p, r, where: (p, 0, 0)),) * 2,
        ),
        compiler_params=pltpu.CompilerParams(vmem_limit_bytes=ROOM),
        cost_estimate=CHEAP,
        name="send_products",
    )(where, *arrays)


def keep_products(where, products, arrived):
    specs, arrays, columns_at = operands(products, 0)
    count, rows, columns = len(products), products[0][1].shape[-2] // 2, products[0][2].shape[1]

    def kernel(where_ref, *refs):
        def use(value):
            for quarter, (arrived_ref, out) in enumerate(zip(refs[-4:-2], refs[-2:])):
                @pl.when(pl.program_id(1) == quarter)
                def _():
                    out[0] = (value + arrived_ref[0].astype(F32)).astype(BF16)
        run_products(refs, columns_at, use)

    return pl.pallas_call(
        kernel,
        out_shape=(jax.ShapeDtypeStruct((count, rows, columns), BF16),) * 2,
        grid_spec=pltpu.PrefetchScalarGridSpec(
            num_scalar_prefetch=1,
            grid=(count, 2),
            in_specs=specs + [pl.BlockSpec((1, rows, columns), lambda p, r, where: (p, 0, 0))] * 2,
            out_specs=(pl.BlockSpec((1, rows, columns), lambda p, r, where: (p, 0, 0)),) * 2,
        ),
        compiler_params=pltpu.CompilerParams(vmem_limit_bytes=ROOM),
        cost_estimate=CHEAP,
        name="keep_products",
    )(where, *arrays, *arrived)


def place(base, parity, kept, arrived, out, shape):
    count = len(kept)
    rows, columns = shape[2], shape[4]
    block = rows // 2

    def kernel(base_ref, *refs):
        out_ref, wide = refs[-2:]
        first = base_ref[1] == 0
        for index in range(count):
            mine, theirs = refs[index][0].astype(F32), refs[count + index][0].astype(F32)
            wide[:, index, :] = jnp.where(first, mine, theirs)
            wide[:, count + index, :] = jnp.where(first, theirs, mine)
        out_ref[0, 0] = wide[...].astype(BF16)

    pieces = kept + arrived
    specs = [
        pl.BlockSpec((1, block, columns), lambda a, i, base, j=j, first=first: (first + a, i, j))
        for _, first, j in pieces]
    extra = [] if out is None else [out]
    return pl.pallas_call(
        kernel,
        out_shape=jax.ShapeDtypeStruct(shape, BF16),
        grid_spec=pltpu.PrefetchScalarGridSpec(
            num_scalar_prefetch=1,
            grid=(2, rows // block),
            in_specs=specs + [pl.BlockSpec(memory_space=pl.ANY)] * len(extra),
            out_specs=pl.BlockSpec(
                (1, 1, block, 2 * count, columns),
                lambda a, i, base: (base[0] + (a + parity) % 2, a, i, 0, 0)),
            scratch_shapes=[pltpu.VMEM((block, 2 * count, columns), F32)],
        ),
        input_output_aliases={1 + 2 * count: 0} if extra else {},
        compiler_params=pltpu.CompilerParams(vmem_limit_bytes=ROOM),
        cost_estimate=CHEAP,
        name="place",
    )(base, *[array for array, _, _ in pieces], *extra)


class Order:
    def __init__(self):
        self.before, self.edge = [], []

    def follow(self, value):
        return after(value, *self.before) if self.before else value

    def step(self, value):
        self.before = [value]
        return value

    def phase(self, *values):
        self.before = self.before + list(values)
        self.edge = self.before

    def open(self, value):
        return after(value, *self.edge) if self.edge else value


class Batch:
    def __init__(self, order, where, *products):
        self.order, self.where, self.products = order, where, products

    def send(self):
        followed = {id(rhs): rhs for _, _, rhs in self.products}
        followed = {key: self.order.follow(rhs) for key, rhs in followed.items()}
        self.products = [(irrep, lhs, followed[id(rhs)]) for irrep, lhs, rhs in self.products]
        parts = send_products(self.where, self.products)
        self.order.step(parts[1])
        self.arrived = [lax.ppermute(part, "ka", OTHER_CORE) for part in parts]

    def keep(self):
        arrived = [self.order.follow(part) for part in self.arrived]
        self.own, self.away = keep_products(self.where, self.products, arrived)
        self.order.step(self.away)

    def swap(self):
        self.other = lax.ppermute(self.order.open(self.away), "ka", OTHER_Y)

    def finish(self):
        total = (self.own.astype(F32) + self.order.open(self.other).astype(F32)).astype(BF16)
        count, rows, columns = total.shape
        return [total[p].reshape(2, rows // 2, columns) for p in range(count)]


def line_local(ladder_amplitudes, ladder_integrals, cycle_amplitudes, cycle_integrals):
    vir, occ, ka = (lax.axis_index(name) for name in ("vir", "occ", "ka"))
    irreps, rows_here, group, depth = cycle_amplitudes.shape
    quarter = group // 4
    columns = cycle_integrals.shape[3]
    at_end = (vir == 0) | (vir == 3)
    where = jnp.bitwise_xor(ka, jnp.array(RELATIVE, jnp.int32))
    order = Order()

    def columns_of(g):
        return order.open(cycle_integrals)[g].reshape(depth, 2 * columns)

    def exchange(inwards, outwards):
        return move(jnp.where(at_end, order.open(inwards), order.open(outwards)), NEIGHBOUR)

    def batch(*products):
        return Batch(order, where, *products)

    def move(value, route):
        return lax.ppermute(order.open(value), "vir", route)

    def cross(*pairs):
        pairs = [(order.open(near), order.open(far)) for near, far in pairs]
        away = jnp.concatenate([jnp.where(occ == 0, far, near) for near, far in pairs])
        return [jnp.where(occ == 0, near, far) for near, far in pairs], lax.ppermute(away, "occ", OTHER_OCC)

    def home(mine, back):
        return jnp.where(at_end, order.open(back), order.open(mine))

    low = jnp.where((occ == 0) | at_end, 0, 2).astype(jnp.int32)
    shape = (8 // 2, rows_here, quarter, 2 * irreps, columns)

    def put(half, j, crossed, out):
        base = order.follow(jnp.stack([low if half == 0 else 2 - low, occ.astype(jnp.int32)]))
        kept = [(pair[0][index], 0, jj) for pair, index, jj in crossed]
        arrived = [(pair[1], 2 * index, jj) for pair, index, jj in crossed]
        return order.step(place(base, j, kept, arrived, out, shape))

    def rows_of(g):
        return order.open(cycle_amplitudes)[g]

    def straight(near, near_in, rows, one=slice(None)):
        own_rows, foreign = (order.open(value) for value in rows)
        first = lax.ppermute(jnp.where(occ == 0, own_rows, foreign), ("vir", "occ"), [(2, 3), (4, 5), (3, 1), (5, 7)])
        second = lax.ppermute(foreign, ("vir", "occ"), [(2, 1), (4, 7)])
        kept = jnp.where(occ == 0, near[..., one], jnp.where(at_end, first, own_rows))
        arrived = jnp.where(occ == 0, near_in[..., one], jnp.where(at_end, second, first))
        return [kept], arrived

    def over(near):
        return lax.ppermute(order.open(near), "occ", [(1, 0)])

    ca = cycle_amplitudes
    ladder_near = move(ladder_amplitudes, NEIGHBOUR)
    ladder_far = move(ladder_amplitudes, MID_TO_MID)
    b0 = columns_of(0)

    order.phase(ladder_near, ladder_far, b0)
    ladder_last = move(ladder_near, MID_TO_MID)
    on_far = move(ladder_far, MID_TO_END)
    b3, b1, b2 = columns_of(3), columns_of(1), columns_of(2)
    rows0 = rows_of(0)

    order.phase(ladder_last, on_far, b3, b1, b2, rows0)
    on_last = move(ladder_last, MID_TO_END)
    own0 = move(b0, MID_TO_MID)
    a0 = move(rows0, END_TO_MID)
    one = batch((3, ca, b3), (1, ca, b1), (2, ca, b2))
    one.send()
    one.keep()

    order.phase(own0, a0, on_last)
    own3 = move(b3, MID_TO_MID)
    swap3 = move(b3, NEIGHBOUR)
    one.swap()
    two = batch((0, ca, own0), (0, a0, own0))
    rows = jnp.concatenate([
        ladder_amplitudes, ladder_near,
        jnp.where(at_end, order.open(on_far), ladder_far), jnp.where(at_end, order.open(on_last), ladder_last)])
    partial_ladder = order.step(jnp.dot(
        order.follow(rows), ladder_integrals, preferred_element_type=F32).astype(BF16))
    plane = jnp.arange(4)
    held = jnp.where(
        plane // 2 == vir // 2, jnp.where(plane == vir, 0, 1), jnp.where((plane == 1) | (plane == 2), 2, 3))
    step = ladder_amplitudes.shape[0]
    partial_ladder = jnp.concatenate([
        lax.dynamic_slice_in_dim(partial_ladder, held[w] * step, step, 0) for w in range(4)])
    ladder_residual = lax.psum_scatter(partial_ladder, ("occ", "ka"), scatter_dimension=0, tiled=True)
    two.send()
    two.keep()
    rows1 = rows_of(1)

    order.phase(own3, swap3, rows1, one.other)
    s3, s1, s2 = one.finish()
    relay3 = move(swap3, MID_TO_MID)
    both3 = exchange(b0, own3)
    two.swap()
    three = batch((3, ca, swap3), (0, ca, b0), (0, a0, b0))
    three.send()
    three.keep()
    rows2 = rows_of(2)

    order.phase(relay3, both3, rows2, two.other)
    f0 = two.finish()
    relay0 = move(both3, MID_TO_MID)
    both4 = exchange(rows1.reshape(b0.shape), relay3)
    three.swap()
    four = batch((0, ca, both3), (3, ca, jnp.where(at_end, order.open(both3), own3)))
    four.send()
    four.keep()

    order.phase(relay0, both4, three.other, f0[1])
    n3, *s0 = three.finish()
    a1 = both4.reshape(a0.shape)
    own1 = move(b1, MID_TO_MID)
    both5 = exchange(rows2.reshape(2, 4, quarter, depth), jnp.concatenate([f0[1], s0[1]])).reshape(b0.shape)
    four.swap()
    five = batch((0, ca, relay0), (0, a0, relay0), (3, ca, jnp.where(at_end, order.open(both4), relay3)))
    five.send()
    five.keep()

    order.phase(own1, both5, four.other, ladder_residual)
    n0, f3 = four.finish()
    a2 = both5.reshape(a0.shape)
    backs = both5.reshape(8, quarter, 2 * columns)
    f0_back, s0_back = backs[0:2], backs[2:4]
    own2 = move(b2, MID_TO_MID)
    swap1 = move(b1, NEIGHBOUR)
    five.swap()
    six = batch((1, ca, own1), (1, a1, own1))
    six.send()
    six.keep()

    order.phase(own2, swap1, five.other)
    *g0, g3 = five.finish()
    relay1 = move(swap1, MID_TO_MID)
    swap2 = move(b2, NEIGHBOUR)
    six.swap()
    seven = batch((2, ca, own2), (2, a2, own2), (1, ca, swap1))
    seven.send()
    seven.keep()

    order.phase(relay1, swap2, six.other)
    f1 = six.finish()
    relay2 = [move(swap2[:, :columns], MID_TO_MID)]
    backs = move(jnp.concatenate([g0[1], f1[1]]), MID_TO_END)
    x03a = cross((s0[0], home(f0[0], f0_back)), (s3, f3))
    seven.swap()
    eight = batch((1, ca, relay1), (1, a1, relay1), (2, ca, swap2))
    eight.send()
    eight.keep()

    order.phase(relay2[0], backs, x03a[1], seven.other)
    *f2, n1 = seven.finish()
    relay2.append(move(swap2[:, columns:], MID_TO_MID))
    g0_back, f1_back = backs[0:2], backs[2:4]
    f2_back = move(f2[1], MID_TO_END)
    x01 = cross((home(n0, s0_back), home(g0[0], g0_back)), (s1, home(f1[0], f1_back)), (n3, g3))
    eight.swap()
    nine = batch((2, ca, relay2[0]), (2, a2, relay2[0]))
    nine.send()
    nine.keep()
    near1_in = over(n1)

    order.phase(relay2[1], f2_back, x01[1], eight.other)
    *g1, n2 = eight.finish()
    nine.swap()
    ten = batch((2, ca, relay2[1]), (2, a2, relay2[1]))
    ten.send()
    ten.keep()
    ten.swap()
    x2a = cross((s2, home(f2[0], f2_back)))
    near2_in = over(n2)
    x1b = straight(n1, near1_in, g1)
    x2b = [straight(n2, near2_in, nine.finish(), slice(0, columns))]
    final = ten.finish()
    order.before = order.before + [final[0]]
    x2b.append(straight(n2, near2_in, final, slice(columns, 2 * columns)))
    out = None
    for j in range(2):
        out = put(0, j, [(x03a, 0, j), (x01, 1, j), (x2a, 0, j), (x03a, 1, j)], out)
    for j in range(2):
        out = put(1, j, [(x01, 0, j), (x1b, 0, j), (x2b[j], 0, 0), (x01, 2, j)], out)
    return ladder_residual, out


def regroup(blocks):
    local_rows = blocks.shape[1]
    first_irrep = lax.axis_index("vir") * local_rows
    pieces = []
    for local_index in range(local_rows):
        permuted = jnp.bitwise_xor(first_irrep + local_index, jnp.arange(8, dtype=jnp.int32))
        pieces.append(jnp.take(blocks[:, local_index], permuted, axis=2))
    stacked = jnp.stack(pieces, axis=1)
    return jnp.transpose(stacked, (3, 1, 2, 0, 4))


def any_local(ladder_amplitudes, ladder_integrals, cycle_amplitudes, cycle_integrals):
    partial_ladder = jnp.dot(
        lax.all_gather(ladder_amplitudes, "vir", axis=0, tiled=True),
        ladder_integrals,
        preferred_element_type=F32,
    )
    summed_ladder = lax.psum_scatter(
        partial_ladder.astype(BF16), ("occ", "ka"), scatter_dimension=0, tiled=True
    )
    partial_cycle = jnp.einsum(
        "gaxk,gkny->gaxny",
        cycle_amplitudes,
        lax.all_gather(cycle_integrals, "vir", axis=2, tiled=True),
        preferred_element_type=F32,
    )
    summed_cycle = lax.psum_scatter(
        partial_cycle.astype(BF16), "ka", scatter_dimension=2, tiled=True
    )
    arranged = regroup(summed_cycle)
    cycle_residual = lax.all_to_all(arranged, "occ", split_axis=0, concat_axis=3, tiled=True)
    return (summed_ladder, cycle_residual)


def solution(mesh):
    line = (mesh.shape["vir"], mesh.shape["occ"], mesh.shape["ka"]) == (4, 2, 4)
    placed = (
        P("vir", ("occ", "ka")),
        P(("occ", "ka"), "vir"),
        P("occ", "vir", None, "ka"),
        P("occ", "ka", "vir", None),
    )
    return jax.shard_map(
        line_local if line else any_local,
        mesh=mesh,
        in_specs=placed,
        out_specs=(P(("occ", "ka"), "vir"), P("occ", "vir", "ka", None, None)),
        check_vma=False,
    )
```
